512 devices in a mesh: wide: 64 (over z, x, core), narrow: 8 (over y).
Axes of the slice: x: 4, y: 8, z: 8, core: 2. Of those that a mesh axis runs over, the one named last changes fastest.
Arguments:
- source: float32 [512, 256, 256], P('wide', 'narrow'), may hold values from -24 to 24
- face_x: float32 [512, 256, 256], P('wide', 'narrow'), may hold values from 0.25 to 4
- face_y: float32 [512, 256, 256], P('wide', 'narrow'), may hold values from 0.25 to 4
- face_z: float32 [512, 256, 256], P('wide', 'narrow'), may hold values from 0.25 to 4
Outputs:
- pressure: float32 [512, 256, 256], P('wide', 'narrow')
- residual: float32 [512, 256, 256], P('wide', 'narrow')
The draws below stay inside these ranges and needn't reach their ends.
All inputs are finite; a program needn't handle non-finite values.
Results may differ from the reference program's by a relative error of at most 0.00035.
Values sent between devices are 32-bit elements; how exact they have to be, the bound alone decides.
A program may use at most 128 MiB of HBM per device.

```python
import math
import jax
import jax.numpy as jnp

CGI = 6
NX = 512
NY = 256
NZ = 256


def draw_source(key, part):
    key = jax.random.fold_in(key, 7)
    along_x = (jnp.arange(NX, dtype=jnp.float32) + 0.5) / NX
    ramp = jnp.exp(math.log(3.0) * along_x)[:, None, None]
    rough = jnp.clip(jax.random.normal(key, (NX, NY, NZ), jnp.float32), -4.0, 4.0)
    return 2.0 * ramp * rough


def level_of(own_key, extent, shards, least, largest):
    def one(dim, parts):
        heights = jax.random.uniform(jax.random.fold_in(jax.random.fold_in(own_key, 6), dim), (parts,), jnp.float32, least / len(shards), largest / len(shards))
        return jnp.repeat(jnp.exp(heights), extent[dim] // parts).reshape((-1,) + (1,) * (len(extent) - dim - 1))

    level = one(*shards[0])
    for cut in shards[1:]:
        level = level * one(*cut)
    return level


def setup_inputs(seed: int = 0) -> dict:
    keys = jax.random.split(jax.random.key(seed), 5)
    source = draw_source(jax.random.fold_in(keys[4], 71), 0)
    face_x = jnp.clip(jnp.exp(math.log(4.0) - 2.7725887 * jax.random.uniform(keys[1], (NX, NY, NZ), jnp.float32) ** level_of(keys[1], (NX, NY, NZ), ((0, 64), (1, 8)), -0.2, 0.2)), 0.25, 4.0)
    face_y = jnp.clip(jnp.exp(math.log(4.0) - 2.7725887 * jax.random.uniform(keys[2], (NX, NY, NZ), jnp.float32) ** level_of(keys[2], (NX, NY, NZ), ((0, 64), (1, 8)), -0.2, 0.2)), 0.25, 4.0)
    face_z = jnp.clip(jnp.exp(math.log(4.0) - 2.7725887 * jax.random.uniform(keys[3], (NX, NY, NZ), jnp.float32) ** level_of(keys[3], (NX, NY, NZ), ((0, 64), (1, 8)), -0.2, 0.2)), 0.25, 4.0)
    return dict(source=source, face_x=face_x, face_y=face_y, face_z=face_z)


relax = 0.8
depth = 3


def pair_sum(array, which):
    shape = array.shape
    folded = shape[:which] + (shape[which] // 2, 2) + shape[which + 1:]
    return jnp.sum(array.reshape(folded), axis=which + 1)


def restrict(remain):
    return pair_sum(pair_sum(pair_sum(remain, 0), 1), 2)


def prolong(coarse):
    return jnp.repeat(jnp.repeat(jnp.repeat(coarse, 2, axis=0), 2, axis=1), 2, axis=2)


def coarsen(faces):
    face_x, face_y, face_z = faces
    return (pair_sum(pair_sum(face_x[1::2], 1), 2),
            pair_sum(pair_sum(face_y[:, 1::2], 0), 2),
            pair_sum(pair_sum(face_z[:, :, 1::2], 0), 1))


def complete(faces):
    face_x, face_y, face_z = faces
    low_x = jnp.concatenate([jnp.zeros_like(face_x[:1]), face_x[:-1]], axis=0)
    low_y = jnp.concatenate([jnp.zeros_like(face_y[:, :1]), face_y[:, :-1]], axis=1)
    low_z = jnp.concatenate([jnp.zeros_like(face_z[:, :, :1]), face_z[:, :, :-1]], axis=2)
    diagonal = face_x + low_x + face_y + low_y + face_z + low_z
    return (face_x, face_y, face_z, low_x, low_y, low_z, diagonal)


def operate(field, coeffs):
    face_x, face_y, face_z, low_x, low_y, low_z, diagonal = coeffs
    padded = jnp.pad(field, 1)
    beside_all = face_x * padded[2:, 1:-1, 1:-1] + low_x * padded[:-2, 1:-1, 1:-1]
    beside_all = beside_all + face_y * padded[1:-1, 2:, 1:-1] + low_y * padded[1:-1, :-2, 1:-1]
    beside_all = beside_all + face_z * padded[1:-1, 1:-1, 2:] + low_z * padded[1:-1, 1:-1, :-2]
    return diagonal * field - beside_all


def conjugate(source, coeffs):
    solved = jnp.zeros_like(source)
    remain = source
    direction = source
    norm_now = jnp.sum(remain * remain)
    for counter in range(CGI):
        image = operate(direction, coeffs)
        alpha = norm_now / jnp.sum(direction * image)
        solved = solved + alpha * direction
        remain = remain - alpha * image
        norm_next = jnp.sum(remain * remain)
        direction = remain + (norm_next / norm_now) * direction
        norm_now = norm_next
    return solved


def cycle(level, source, faces):
    coeffs = complete(faces)
    diagonal = coeffs[6]
    field = relax * source / diagonal
    field = field + relax * (source - operate(field, coeffs)) / diagonal
    remain = source - operate(field, coeffs)
    coarse_source = restrict(remain)
    coarse_faces = coarsen(faces)
    if level + 1 == depth:
        correction = conjugate(coarse_source, complete(coarse_faces))
    else:
        correction = cycle(level + 1, coarse_source, coarse_faces)[0]
    field = field + prolong(correction)
    for sweeping in range(2):
        field = field + relax * (source - operate(field, coeffs)) / diagonal
    return field, coeffs


def reference(source, face_x, face_y, face_z):
    pressure, coeffs = cycle(0, source, (face_x, face_y, face_z))
    residual = source - operate(pressure, coeffs)
    return pressure, residual
```

```python
import functools

import jax
import jax.numpy as jnp
from jax import lax
from jax.experimental import pallas as pl
from jax.experimental.pallas import tpu as pltpu
from jax.sharding import PartitionSpec as P

CGI = 6
relax = 0.8
MESH = pl.DeviceIdType.MESH
F32 = jnp.float32
BF16 = jnp.bfloat16


def iota(shape, dim):
    return lax.broadcasted_iota(jnp.int32, shape, dim)


def picked(values, chosen):
    high = values.astype(BF16)
    rest = values - high.astype(F32)
    middle = rest.astype(BF16)
    low = (rest - middle.astype(F32)).astype(BF16)
    product = functools.partial(jnp.dot, preferred_element_type=F32)
    return product(high, chosen) + product(middle, chosen) + product(low, chosen)


def ones_where(condition):
    return jnp.where(condition, 1.0, 0.0).astype(BF16)


def next_z(cells):
    lanes = cells.shape[-1]
    lane = iota(cells.shape[:-1] + (128,), len(cells.shape) - 1)
    axis = len(cells.shape) - 1
    if lanes == 128:
        return jnp.where(lane == 127, 0.0, pltpu.roll(cells, 127, axis))
    first = pltpu.roll(cells[..., :128], 127, axis)
    second = pltpu.roll(cells[..., 128:], 127, axis)
    return jnp.concatenate([jnp.where(lane == 127, second, first), jnp.where(lane == 127, 0.0, second)], axis=axis)


def last_z(cells):
    lanes = cells.shape[-1]
    lane = iota(cells.shape[:-1] + (128,), len(cells.shape) - 1)
    axis = len(cells.shape) - 1
    if lanes == 128:
        return jnp.where(lane == 0, 0.0, pltpu.roll(cells, 1, axis))
    first = pltpu.roll(cells[..., :128], 1, axis)
    second = pltpu.roll(cells[..., 128:], 1, axis)
    return jnp.concatenate([jnp.where(lane == 0, 0.0, first), jnp.where(lane == 0, first, second)], axis=axis)


def remainder(b, f, v, p):
    here = v[p]
    rows = here.shape[0]
    flow = f[0, p] * (v[p + 1] - here) - f[0, p - 1] * (here - v[p - 1])
    along = f[1, p] * (pltpu.roll(here, rows - 1, 0) - here)
    flow = flow + (along - pltpu.roll(along, 1, 0))
    along = f[2, p] * (next_z(here) - here)
    flow = flow + (along - last_z(along))
    return b[p] + flow


def diagonal(f, p):
    return (f[0, p] + f[0, p - 1]) + (f[1, p] + pltpu.roll(f[1, p], 1, 0)) + (f[2, p] + last_z(f[2, p]))


def body(sizes, src, inx, iny, inz, out_p, out_r, IN, PKs, FYs, FYr, RK, W0, VA, VD, VB, VY, VE, VF, RZ, U0,
         F1, F1S, B1, B1S, W1, X1, Y1, Y1R, Y1S, Z1, U1, F2, F2S, B2, B2S, W2, X2, Y2, Y2R, Y2S, Z2,
         T3s, T3r, G3f, B3s, B3r, G3b, EG, YG, ZG, PD, RR, QQ, XS, send_sem, recv_sem, load_sem, store_sem):
    wide, narrow, ring, group = sizes
    i, j = lax.axis_index("wide"), lax.axis_index("narrow")
    zi, ri = lax.div(i, group), lax.rem(i, group)

    def wide_at(step):
        return lax.rem(i + (step + wide), wide)

    def narrow_at(step):
        return lax.rem(j + (step + narrow), narrow)

    loads = []
    for number, ref in enumerate((inx, iny, inz, src)):
        loads.append(pltpu.make_async_copy(ref, IN.at[number, pl.ds(3, 8), pl.ds(0, 32)], load_sem.at[number]))
        loads[-1].start()

    barrier = pltpu.get_barrier_semaphore()
    partners = [(wide_at(a), narrow_at(b)) for a in range(-2, 3) for b in range(-1, 2) if (a, b) != (0, 0)]
    partners += [(i, narrow_at(d)) for d in range(2, narrow - 1)]
    partners += [(lax.rem(zi + d, ring) * group + ri, j) for d in range(1, ring)]
    partners += [(zi * group + lax.rem(ri + d, group), j) for d in range(1, group)]
    for partner in partners:
        pl.semaphore_signal(barrier, inc=1, device_id=partner, device_id_type=MESH)

    sent = []

    def send(source, target, partner):
        number = len(sent)
        copy = pltpu.make_async_remote_copy(
            src_ref=source, dst_ref=target, send_sem=send_sem.at[number], recv_sem=recv_sem.at[number],
            device_id=partner, device_id_type=MESH)
        copy.start()
        sent.append(copy)
        return copy

    def arrive(copies):
        for copy in copies:
            copy.wait_recv()

    def exchange(source, target, stage, own, rows, far):
        near, later = [], []
        for a in sorted(range(-far, far + 1), key=abs):
            for b in (0, 1, -1):
                if (a, b) == (0, 0):
                    continue
                start = 4 - a * own
                low, high = max(start, 0), min(start + own, 8 + own)
                from_low = 4 + low - start
                partner = (wide_at(-a), narrow_at(-b))
                if b == 0:
                    piece = source.at[:, pl.ds(4, own), pl.ds(0, rows)]
                    place = target.at[:, pl.ds(4 + a * own, own), pl.ds(0, rows)]
                else:
                    piece = source.at[:, pl.ds(4, own), pl.ds(rows - 8 if b == -1 else 0, 8)]
                    place = stage.at[0 if b == -1 else 1, :, pl.ds(4 + a * own, own)]
                copy = send(piece, place, partner)
                (near if abs(a) < 2 else later).append(copy)
        return near, later

    tile_row = iota((8, 128), 0)
    row256 = iota((8, 256), 0)

    def merged(stage, field, plane):
        return jnp.where(tile_row < 4, stage[1, field, plane], stage[0, field, plane])

    for copy in loads:
        copy.wait()

    @pl.loop(0, 8)
    def pack(p):
        up = jnp.zeros((8, 256), F32)
        down = jnp.zeros((8, 256), F32)
        for f in range(4):
            mine = (row256 >> 1) == f
            up = jnp.where(mine, pltpu.roll(IN[f, 3 + p, 24:32], (2 * f + 2) % 8, 0), up)
            down = jnp.where(mine, pltpu.roll(IN[f, 3 + p, 0:8], 2 * f, 0), down)
        PKs[0, p] = up
        PKs[1, p] = down

    for p in range(8):
        FYs[p:p + 1] = IN[1, 3 + p, 29:30]

    pl.semaphore_wait(barrier, len(partners))

    first = []
    first.append(send(IN.at[:, pl.ds(9, 2), pl.ds(0, 32)], IN.at[:, pl.ds(1, 2), pl.ds(0, 32)], (wide_at(1), j)))
    first.append(send(IN.at[:, pl.ds(3, 2), pl.ds(0, 32)], IN.at[:, pl.ds(11, 2), pl.ds(0, 32)], (wide_at(-1), j)))
    first.append(send(IN.at[0, pl.ds(8, 1), pl.ds(0, 32)], IN.at[0, pl.ds(0, 1), pl.ds(0, 32)], (wide_at(1), j)))
    for side, b in ((0, 1), (1, -1)):
        first.append(send(PKs.at[side], RK.at[side, pl.ds(2, 8)], (i, narrow_at(b))))
        first.append(send(PKs.at[side, pl.ds(6, 2)], RK.at[side, pl.ds(0, 2)], (wide_at(1), narrow_at(b))))
        first.append(send(PKs.at[side, pl.ds(0, 2)], RK.at[side, pl.ds(10, 2)], (wide_at(-1), narrow_at(b))))
    first.append(send(FYs, FYr, (i, narrow_at(1))))

    pairs0 = ones_where((iota((256, 128), 0) >> 1) == iota((256, 128), 1))
    odds0 = ones_where(iota((256, 128), 0) == 2 * iota((256, 128), 1) + 1)
    pairs1 = ones_where((iota((128, 128), 0) >> 1) == iota((128, 128), 1))
    odds1 = ones_where(iota((128, 128), 0) == 2 * iota((128, 128), 1) + 1)
    pairs2 = ones_where((iota((128, 128), 0) >> 1) == (iota((128, 128), 1) & 31))
    odds2 = ones_where(iota((128, 128), 0) == 2 * (iota((128, 128), 1) & 31) + 1)

    def paired(tiles, odd_only=False):
        lanes = tiles[0].shape[1]
        half = tiles[0].shape[0] // 2
        for c, tile in enumerate(tiles):
            for part in range(lanes // 128):
                RZ[part, c, 0:2 * half] = tile[:, 128 * part:128 * (part + 1)]
        below = []
        for c in range(len(tiles)):
            beside = []
            for part in range(lanes // 128):
                odd = RZ[part, c, pl.ds(1, half, stride=2), :]
                beside.append(odd if odd_only else RZ[part, c, pl.ds(0, half, stride=2), :] + odd)
            below.append(jnp.concatenate(beside, axis=1) if len(beside) > 1 else beside[0])
        return jnp.concatenate(below, axis=0)

    def coarse_faces(f, at, target, own, rows, pairs, odds):
        half = rows // 2
        x = [f[0, at + 2 * c + 1, 0:rows] for c in range(own)]
        y = [f[1, at + 2 * c, 0:rows] + f[1, at + 2 * c + 1, 0:rows] for c in range(own)]
        z = [f[2, at + 2 * c, 0:rows] + f[2, at + 2 * c + 1, 0:rows] for c in range(own)]
        for number, (tiles, odd_only, chosen) in enumerate(((x, False, pairs), (y, True, pairs), (z, False, odds))):
            got = picked(paired(tiles, odd_only), chosen)
            for c in range(own):
                target[number, 4 + c, 0:half] = got[c * half:(c + 1) * half]

    coarse_faces(IN, 3, F1, 4, 32, pairs0, odds0)
    faces1, _ = exchange(F1, F1, F1S, 4, 16, 1)
    coarse_faces(F1, 4, F2, 2, 16, pairs1, odds1)
    near, later = exchange(F2, F2, F2S, 2, 8, 2)
    faces2 = near + later

    lane_block = iota((8, 128), 1) >> 5
    both_rows = (tile_row >> 1) == lane_block
    odd_rows = tile_row == 2 * lane_block + 1

    def to_row(tile, chosen, mask):
        got = jnp.where(mask, picked(tile, chosen), 0.0)
        return jnp.broadcast_to(jnp.sum(got, axis=0, keepdims=True), (narrow, 128))

    T3s[0] = to_row(F2[0, 5, 0:8], pairs2, both_rows)
    T3s[1] = to_row(F2[1, 4, 0:8] + F2[1, 5, 0:8], pairs2, odd_rows)
    T3s[2] = to_row(F2[2, 4, 0:8] + F2[2, 5, 0:8], odds2, both_rows)
    gather_f = [send(T3s, T3r.at[j], (i, narrow_at(d))) for d in range(1, narrow)]
    T3r[j] = T3s[...]

    arrive(first)
    has_low, has_high = j > 0, j < narrow - 1

    @pl.loop(0, 12)
    def unpack(q):
        low, high = RK[0, q], RK[1, q]
        for f in range(4):
            from_high = pltpu.roll(high, (8 - 2 * f) % 8, 0)
            from_low = pltpu.roll(low, (14 - 2 * f) % 8, 0)
            if f == 1:
                from_low = jnp.where(has_low, from_low, 0.0)
            IN[f, q + 1, 32:40] = jnp.where(row256 < 2, from_high, jnp.where(row256 >= 6, from_low, 0.0))

    IN[0, 0, 32:40] = jnp.zeros((8, 256), F32)
    for p in range(8):
        IN[1, 3 + p, 37:38] = jnp.where(has_low, FYr[p:p + 1], 0.0)

    @pl.when(i == 0)
    def _():
        IN[0, 2] = jnp.zeros((40, 256), F32)

    def inside(rows, lanes, own_rows, reach):
        row = iota((rows, lanes), 0)
        mask = (row < own_rows) | ((row < own_rows + reach) & has_high) | ((row >= rows - reach) & has_low)
        return mask

    def plane_in(p, own):
        return (i * own + p >= 0) & (i * own + p < own * wide)

    rows_in0 = inside(40, 256, 32, 2)
    weight_in = jnp.where(rows_in0, relax, 0.0)

    @pl.loop(-2, 10)
    def start0(p):
        w = jnp.where(plane_in(p, 8), weight_in, 0.0) / diagonal(IN, p + 3)
        W0[p + 3] = w
        VA[p + 3] = w * IN[3, p + 3]

    @pl.loop(-1, 9)
    def down0(p):
        VD[p + 3] = VA[p + 3] + W0[p + 3] * remainder(IN.at[3], IN, VA, p + 3)

    background = []
    background.append(send(VD.at[pl.ds(8, 3), pl.ds(0, 32)], VB.at[pl.ds(0, 3)], (wide_at(1), j)))
    background.append(send(VD.at[pl.ds(3, 3), pl.ds(0, 32)], VB.at[pl.ds(3, 3)], (wide_at(-1), j)))
    for side, b, row in ((0, 1, 24), (1, -1, 0)):
        background.append(send(VD.at[pl.ds(3, 8), pl.ds(row, 8)], VY.at[side, pl.ds(3, 8)], (i, narrow_at(b))))
        background.append(send(VD.at[pl.ds(8, 3), pl.ds(row, 8)], VY.at[side, pl.ds(0, 3)], (wide_at(1), narrow_at(b))))
        background.append(send(VD.at[pl.ds(3, 3), pl.ds(row, 8)], VY.at[side, pl.ds(11, 3)], (wide_at(-1), narrow_at(b))))

    @pl.loop(0, 4)
    def restrict0(c):
        VE[c, 0:32] = remainder(IN.at[3], IN, VD, 2 * c + 3)[:32] + remainder(IN.at[3], IN, VD, 2 * c + 4)[:32]

    got = paired([VE[c, 0:32] for c in range(4)])
    got = picked(got, pairs0)
    for c in range(4):
        B1[0, 4 + c, 0:16] = got[16 * c:16 * (c + 1)]
    rhs1, _ = exchange(B1, B1, B1S, 4, 16, 1)

    arrive(gather_f)
    sub = iota((narrow, 128), 0)

    def assembled(parts):
        tile = parts[0]
        for n in range(1, narrow):
            tile = jnp.where(sub == n, parts[n], tile)
        return tile

    for f in range(3):
        G3f[f, zi, ri] = assembled([T3r[n, f] for n in range(narrow)])
    gather_f = [send(G3f.at[:, zi, ri], G3f.at[:, zi, ri], (lax.rem(zi + d, ring) * group + ri, j)) for d in range(1, ring)]

    def finish_faces(f, stage, planes, rows):
        for p in range(planes):
            for field in range(3):
                tile = merged(stage, field, p)
                if field == 1:
                    tile = jnp.where((tile_row < 4) | has_low, tile, 0.0)
                f[field, p, rows:rows + 8] = tile

        @pl.when(i == 0)
        def _():
            f[0, 3] = jnp.zeros(f.shape[2:], F32)

        if planes == 10:
            @pl.when(i == 1)
            def _():
                f[0, 1] = jnp.zeros(f.shape[2:], F32)

    arrive(faces1)
    finish_faces(F1, F1S, 12, 16)
    rows_in1 = inside(24, 128, 16, 4)
    weight_in1 = jnp.where(rows_in1, relax, 0.0)

    @pl.loop(-3, 8)
    def weights1(p):
        W1[p + 4] = jnp.where(plane_in(p, 4), weight_in1, 0.0) / diagonal(F1, p + 4)

    arrive(rhs1)
    for p in range(12):
        B1[0, p, 16:24] = merged(B1S, 0, p)

    @pl.loop(-2, 6)
    def start1(p):
        X1[p + 4] = W1[p + 4] * B1[0, p + 4]

    @pl.loop(-1, 5)
    def down1(p):
        Y1[0, p + 4] = X1[p + 4] + W1[p + 4] * remainder(B1.at[0], F1, X1, p + 4)

    back1, _ = exchange(Y1, Y1R, Y1S, 4, 16, 1)
    got = paired([remainder(B1.at[0], F1, Y1.at[0], 2 * c + 4)[:16] + remainder(B1.at[0], F1, Y1.at[0], 2 * c + 5)[:16]
                  for c in range(2)])
    got = picked(got, pairs1)
    for c in range(2):
        B2[0, 4 + c, 0:8] = got[8 * c:8 * (c + 1)]
    rhs2, rhs2_far = exchange(B2, B2, B2S, 2, 8, 2)

    arrive(gather_f)
    gather_f = [send(G3f.at[:, :, ri], G3f.at[:, :, ri], (zi * group + lax.rem(ri + d, group), j)) for d in range(1, group)]

    arrive(faces2)
    finish_faces(F2, F2S, 10, 8)
    rows_in2 = inside(16, 128, 8, 4) & (iota((16, 128), 1) < 64)

    @pl.loop(-3, 6)
    def weights2(p):
        W2[p + 4] = jnp.where(rows_in2 & plane_in(p, 2), relax / diagonal(F2, p + 4), 0.0)

    arrive(rhs2)
    for p in range(2, 8):
        B2[0, p, 8:16] = merged(B2S, 0, p)

    for p in range(-2, 4):
        X2[p + 4] = W2[p + 4] * B2[0, p + 4]
    for p in range(-1, 3):
        Y2[0, p + 4] = X2[p + 4] + W2[p + 4] * remainder(B2.at[0], F2, X2, p + 4)
    back2_near, back2_far = exchange(Y2, Y2R, Y2S, 2, 8, 2)
    got = remainder(B2.at[0], F2, Y2.at[0], 4)[:8] + remainder(B2.at[0], F2, Y2.at[0], 5)[:8]
    B3s[...] = to_row(got, pairs2, both_rows)
    gather_b = [send(B3s, B3r.at[j], (i, narrow_at(d))) for d in range(1, narrow)]
    B3r[j] = B3s[...]
    arrive(gather_b)
    G3b[zi, ri] = assembled([B3r[n] for n in range(narrow)])
    gather_b = [send(G3b.at[zi, ri], G3b.at[zi, ri], (lax.rem(zi + d, ring) * group + ri, j)) for d in range(1, ring)]

    arrive(gather_f)
    block3 = iota((narrow, 128), 1) >> 5
    lane3 = iota((narrow, 128), 1) & 31
    last_y = (sub == narrow - 1) & (block3 == 3)
    last_lane = lane3 == 31

    @pl.loop(0, wide)
    def masks3(p):
        a, b = lax.div(p, group), lax.rem(p, group)
        y, z = G3f[1, a, b], G3f[2, a, b]
        EG[p] = jnp.where(last_y, y, 0.0) + jnp.where(last_lane, z, 0.0)
        YG[p] = jnp.where(last_y, 0.0, y)
        ZG[p] = jnp.where(last_lane, 0.0, z)

    arrive(gather_b)
    gather_b = [send(G3b.at[:, ri], G3b.at[:, ri], (zi * group + lax.rem(ri + d, group), j)) for d in range(1, group)]
    for p in (0, 1, wide + 2, wide + 3):
        PD[p] = jnp.zeros((narrow, 128), F32)
    for p in range(5):
        XS[p] = jnp.zeros((narrow, 128), F32)
    arrive(gather_b)

    zero3 = jnp.zeros((narrow, 128), F32)

    def next_y3(cells):
        moved = pltpu.roll(cells, 96, 1)
        return jnp.where(block3 == 3, pltpu.roll(moved, narrow - 1, 0), moved)

    def last_y3(cells):
        moved = pltpu.roll(cells, 32, 1)
        return jnp.where(block3 == 0, pltpu.roll(moved, 1, 0), moved)

    def begin(a, total):
        for b in range(group):
            p = a * group + b
            r = G3b[a, b]
            PD[p + 2] = r
            RR[p] = r
            total = total + r * r
        return total

    def summed(total):
        return jnp.sum(jnp.sum(total, axis=0, keepdims=True), axis=1, keepdims=True)

    def image(a, carry):
        total, low = carry
        for b in range(group):
            p = a * group + b
            here = PD[p + 2]
            high = G3f[0, a, b] * (here - PD[p + 3])
            along_y = YG[p] * (here - next_y3(here))
            along_z = ZG[p] * (here - pltpu.roll(here, 127, 1))
            q = (EG[p] * here + (high - low)) + ((along_y - last_y3(along_y)) + (along_z - pltpu.roll(along_z, 1, 1)))
            QQ[p] = q
            total = total + here * q
            low = high
        return total, low

    norm_now = summed(lax.fori_loop(0, ring, begin, zero3))
    for counter in range(CGI):
        total, _ = lax.fori_loop(0, ring, image, (zero3, zero3))
        alpha = norm_now / summed(total)
        for p in range(5):
            XS[p] = XS[p] + alpha * PD[i + p]
        if counter == CGI - 1:
            break

        def descend(a, total, alpha=alpha):
            for b in range(group):
                p = a * group + b
                r = RR[p] - alpha * QQ[p]
                RR[p] = r
                total = total + r * r
            return total

        norm_next = summed(lax.fori_loop(0, ring, descend, zero3))
        beta = norm_next / norm_now

        def turn(a, carry, beta=beta):
            for b in range(group):
                p = a * group + b
                PD[p + 2] = RR[p] + beta * PD[p + 2]
            return carry

        lax.fori_loop(0, ring, turn, 0)
        norm_now = norm_next

    row16 = iota((16, 128), 0)
    wanted = ((row16 & 7) >> 1) == (iota((16, 128), 1) >> 5)
    spread2 = ones_where(((iota((128, 128), 1) >> 1) == (iota((128, 128), 0) & 31)) & (iota((128, 128), 1) < 64))
    high_j, low_j = jnp.minimum(j + 1, narrow - 1), jnp.maximum(j - 1, 0)
    spread = []
    for p in range(5):
        middle = jnp.broadcast_to(XS[p, pl.ds(j, 1), :], (16, 128))
        above = jnp.broadcast_to(XS[p, pl.ds(high_j, 1), :], (16, 128))
        below = jnp.broadcast_to(XS[p, pl.ds(low_j, 1), :], (16, 128))
        x = jnp.where(row16 < 8, middle, jnp.where(row16 < 12, above, below))
        spread.append(jnp.where(wanted, x, 0.0))
    spread = picked(jnp.concatenate(spread, axis=0), spread2)
    arrive(rhs2_far + back2_near + back2_far)
    reach2 = inside(16, 128, 8, 4)
    for p in (0, 1, 8, 9):
        B2[0, p, 8:16] = merged(B2S, 0, p)
    for p in range(-4, 6):
        own = Y2[0, p + 4, 0:8] if 0 <= p < 2 else Y2R[0, p + 4, 0:8]
        x = jnp.concatenate([own, merged(Y2S, 0, p + 4)], axis=0)
        c = (p + 4) // 2
        x = x + spread[16 * c:16 * (c + 1)]
        X2[p + 4] = jnp.where(reach2 & plane_in(p, 2), x, 0.0)
    for p in range(-3, 5):
        Z2[p + 4] = X2[p + 4] + W2[p + 4] * remainder(B2.at[0], F2, X2, p + 4)
    for p in range(-2, 4):
        X2[p + 4] = Z2[p + 4] + W2[p + 4] * remainder(B2.at[0], F2, Z2, p + 4)

    spread1 = ones_where((iota((128, 128), 1) >> 1) == iota((128, 128), 0))
    spread = picked(jnp.concatenate([X2[p + 4] for p in range(-2, 4)], axis=0), spread1)
    for c in range(6):
        U1[c, pl.ds(0, 16, stride=2), :] = spread[16 * c:16 * (c + 1)]
        U1[c, pl.ds(1, 16, stride=2), :] = spread[16 * c:16 * (c + 1)]
    arrive(back1)
    reach1 = inside(24, 128, 16, 4)
    for p in range(-4, 8):
        c = (p + 4) // 2
        own = Y1[0, p + 4, 0:16] if 0 <= p < 4 else Y1R[0, p + 4, 0:16]
        edge = merged(Y1S, 0, p + 4) + jnp.where(tile_row < 4, U1[c, 16:24], U1[c, 24:32])
        x = jnp.concatenate([own + U1[c, 0:16], edge], axis=0)
        X1[p + 4] = jnp.where(reach1 & plane_in(p, 4), x, 0.0)

    @pl.loop(-3, 7)
    def up1(p):
        Z1[p + 4] = X1[p + 4] + W1[p + 4] * remainder(B1.at[0], F1, X1, p + 4)

    @pl.loop(-2, 6)
    def up1_again(p):
        X1[p + 4] = Z1[p + 4] + W1[p + 4] * remainder(B1.at[0], F1, Z1, p + 4)

    spread0 = ones_where((iota((128, 256), 1) >> 1) == iota((128, 256), 0))
    spread = picked(jnp.concatenate([X1[p + 4] for p in range(-2, 6)], axis=0), spread0)
    for c in range(8):
        for half in (0, 128):
            part = spread[24 * c:24 * (c + 1), half:half + 128]
            U0[half // 128, c, pl.ds(0, 24, stride=2), :] = part
            U0[half // 128, c, pl.ds(1, 24, stride=2), :] = part
    arrive(background)
    reach0 = inside(40, 256, 32, 4)

    def corrected(p, own):
        c = lax.div(p + 4, 2)
        u = jnp.concatenate([U0[0, c], U0[1, c]], axis=1)
        edge = jnp.where(row256 < 4, VY[1, p + 3] + u[32:40], VY[0, p + 3] + u[40:48])
        x = jnp.concatenate([own + u[0:32], edge], axis=0)
        return jnp.where(reach0 & plane_in(p, 8), x, 0.0)

    @pl.loop(0, 8)
    def correct0(p):
        VE[p + 3] = corrected(p, VD[p + 3, 0:32])

    @pl.loop(0, 3)
    def correct0_ends(p):
        VE[p] = corrected(p - 3, VB[p])
        VE[p + 11] = corrected(p + 8, VB[p + 3])

    @pl.loop(-2, 10)
    def up0(p):
        VA[p + 3] = VE[p + 3] + W0[p + 3] * remainder(IN.at[3], IN, VE, p + 3)

    @pl.loop(-1, 9)
    def up0_again(p):
        VF[p + 3] = VA[p + 3] + W0[p + 3] * remainder(IN.at[3], IN, VA, p + 3)

    store = pltpu.make_async_copy(VF.at[pl.ds(3, 8), pl.ds(0, 32)], out_p, store_sem.at[0])
    store.start()

    @pl.loop(0, 8)
    def rest0(p):
        VE[p] = remainder(IN.at[3], IN, VF, p + 3)

    store_r = pltpu.make_async_copy(VE.at[pl.ds(0, 8), pl.ds(0, 32)], out_r, store_sem.at[1])
    store_r.start()
    for copy in sent:
        copy.wait_send()
    store.wait()
    store_r.wait()


def shards(sizes, source, face_x, face_y, face_z):
    wide, narrow, ring, group = sizes
    shape = jax.ShapeDtypeStruct((8, 32, 256), F32)

    def V(*size):
        return pltpu.VMEM(size, F32)

    scratch = [
        V(4, 13, 40, 256), V(2, 8, 8, 256), V(8, 256), V(8, 256), V(2, 12, 8, 256),
        V(14, 40, 256), V(14, 40, 256), V(14, 40, 256), V(6, 32, 256), V(2, 14, 8, 256), V(14, 40, 256), V(14, 40, 256),
        V(2, 4, 32, 128), V(2, 8, 48, 128),
        V(3, 12, 24, 128), V(2, 3, 12, 8, 128), V(1, 12, 24, 128), V(2, 1, 12, 8, 128), V(12, 24, 128), V(12, 24, 128),
        V(1, 12, 24, 128), V(1, 12, 24, 128), V(2, 1, 12, 8, 128), V(12, 24, 128), V(6, 32, 128),
        V(3, 10, 16, 128), V(2, 3, 10, 8, 128), V(1, 10, 16, 128), V(2, 1, 10, 8, 128), V(10, 16, 128), V(10, 16, 128),
        V(1, 10, 16, 128), V(1, 10, 16, 128), V(2, 1, 10, 8, 128), V(10, 16, 128),
        V(3, narrow, 128), V(narrow, 3, narrow, 128), V(3, ring, group, narrow, 128),
        V(narrow, 128), V(narrow, narrow, 128), V(ring, group, narrow, 128), V(wide, narrow, 128),
        V(wide, narrow, 128), V(wide, narrow, 128),
        V(wide + 4, narrow, 128), V(wide, narrow, 128), V(wide, narrow, 128), V(5, narrow, 128),
        pltpu.SemaphoreType.DMA((144,)), pltpu.SemaphoreType.DMA((144,)), pltpu.SemaphoreType.DMA((4,)),
        pltpu.SemaphoreType.DMA((2,)),
    ]
    anywhere = pl.BlockSpec(memory_space=pl.ANY)
    return pl.pallas_call(
        functools.partial(body, sizes),
        out_shape=(shape, shape),
        in_specs=[anywhere] * 4,
        out_specs=(anywhere, anywhere),
        scratch_shapes=scratch,
        compiler_params=pltpu.CompilerParams(collective_id=0, has_side_effects=True, vmem_limit_bytes=40 * 1024 * 1024),
    )(source, face_x, face_y, face_z)


def solution(mesh):
    wide, narrow = mesh.shape["wide"], mesh.shape["narrow"]
    group = 8 if wide == 64 else wide // 2
    spec = P("wide", "narrow", None)
    return jax.shard_map(
        functools.partial(shards, (wide, narrow, wide // group, group)),
        mesh=mesh,
        in_specs=(spec,) * 4,
        out_specs=(spec, spec),
        check_vma=False,
    )
```

```python
import functools

import jax
import jax.numpy as jnp
from jax import lax
from jax.experimental import pallas as pl
from jax.experimental.pallas import tpu as pltpu
from jax.sharding import PartitionSpec as P

CGI = 6
relax = 0.8
MESH = pl.DeviceIdType.MESH
F32 = jnp.float32
BF16 = jnp.bfloat16


def iota(shape, dim):
    return lax.broadcasted_iota(jnp.int32, shape, dim)


def picked(values, chosen):
    high = values.astype(BF16)
    rest = values - high.astype(F32)
    middle = rest.astype(BF16)
    low = (rest - middle.astype(F32)).astype(BF16)
    product = functools.partial(jnp.dot, preferred_element_type=F32)
    return product(high, chosen) + product(middle, chosen) + product(low, chosen)


def ones_where(condition):
    return jnp.where(condition, 1.0, 0.0).astype(BF16)


def next_z(cells):
    lanes = cells.shape[-1]
    lane = iota(cells.shape[:-1] + (128,), len(cells.shape) - 1)
    axis = len(cells.shape) - 1
    if lanes == 128:
        return jnp.where(lane == 127, 0.0, pltpu.roll(cells, 127, axis))
    first = pltpu.roll(cells[..., :128], 127, axis)
    second = pltpu.roll(cells[..., 128:], 127, axis)
    return jnp.concatenate([jnp.where(lane == 127, second, first), jnp.where(lane == 127, 0.0, second)], axis=axis)


def last_z(cells):
    lanes = cells.shape[-1]
    lane = iota(cells.shape[:-1] + (128,), len(cells.shape) - 1)
    axis = len(cells.shape) - 1
    if lanes == 128:
        return jnp.where(lane == 0, 0.0, pltpu.roll(cells, 1, axis))
    first = pltpu.roll(cells[..., :128], 1, axis)
    second = pltpu.roll(cells[..., 128:], 1, axis)
    return jnp.concatenate([jnp.where(lane == 0, 0.0, first), jnp.where(lane == 0, first, second)], axis=axis)


def remainder(b, f, v, p, n=1):
    here = v[pl.ds(p, n)]
    rows = here.shape[1]
    flow = f[0, pl.ds(p, n)] * (v[pl.ds(p + 1, n)] - here) - f[0, pl.ds(p - 1, n)] * (here - v[pl.ds(p - 1, n)])
    along = f[1, pl.ds(p, n)] * (pltpu.roll(here, rows - 1, 1) - here)
    flow = flow + (along - pltpu.roll(along, 1, 1))
    along = f[2, pl.ds(p, n)] * (next_z(here) - here)
    flow = flow + (along - last_z(along))
    return b[pl.ds(p, n)] + flow


def diagonal(f, p, n=1):
    x, y, z = f[0, pl.ds(p, n)], f[1, pl.ds(p, n)], f[2, pl.ds(p, n)]
    return (x + f[0, pl.ds(p - 1, n)]) + (y + pltpu.roll(y, 1, 1)) + (z + last_z(z))


def sweep(target, v, b, f, w, p, n):
    target[pl.ds(p, n)] = v[pl.ds(p, n)] + w[pl.ds(p, n)] * remainder(b, f, v, p, n)


def body(sizes, src, inx, iny, inz, out_p, out_r, IN, PKs, FYs, FYr, RK, W0, VA, VD, VB, VY, VE, VF, RZ, U0,
         F1, F1S, B1, B1S, W1, X1, Y1, Y1R, Y1S, Z1, U1, F2, F2S, B2, B2S, W2, X2, Y2, Y2R, Y2S, Z2,
         T3s, T3r, G3f, B3s, B3r, G3b, EG, XG, YG, ZG, PD, RR, QQ, XS, send_sem, recv_sem, load_sem, store_sem):
    wide, narrow, ring, group = sizes
    i, j = lax.axis_index("wide"), lax.axis_index("narrow")
    zi, ri = lax.div(i, group), lax.rem(i, group)

    def wide_at(step):
        return lax.rem(i + (step + wide), wide)

    def narrow_at(step):
        return lax.rem(j + (step + narrow), narrow)

    loads = []
    for number, ref in enumerate((inx, iny, inz, src)):
        loads.append(pltpu.make_async_copy(ref, IN.at[number, pl.ds(3, 8), pl.ds(0, 32)], load_sem.at[number]))
        loads[-1].start()

    barrier = pltpu.get_barrier_semaphore()
    partners = [(wide_at(a), narrow_at(b)) for a in (0, 1, -1, 2, -2) for b in (0, 1, -1) if (a, b) != (0, 0)]
    partners += [(i, narrow_at(d)) for d in range(2, narrow - 1)]
    partners += [(lax.rem(zi + d, ring) * group + ri, j) for d in range(1, ring)]
    partners += [(zi * group + lax.rem(ri + d, group), j) for d in range(1, group)]
    for partner in partners:
        pl.semaphore_signal(barrier, inc=1, device_id=partner, device_id_type=MESH)

    sent = []

    def send(source, target, partner):
        number = len(sent)
        copy = pltpu.make_async_remote_copy(
            src_ref=source, dst_ref=target, send_sem=send_sem.at[number], recv_sem=recv_sem.at[number],
            device_id=partner, device_id_type=MESH)
        copy.start()
        sent.append(copy)
        return copy

    def arrive(copies):
        for copy in copies:
            copy.wait_recv()

    def exchange(source, target, stage, own, rows, far):
        near, later = [], []
        for a in sorted(range(-far, far + 1), key=abs):
            for b in (0, 1, -1):
                if (a, b) == (0, 0):
                    continue
                start = 4 - a * own
                low, high = max(start, 0), min(start + own, 8 + own)
                from_low = 4 + low - start
                partner = (wide_at(-a), narrow_at(-b))
                if b == 0:
                    piece = source.at[:, pl.ds(4, own), pl.ds(0, rows)]
                    place = target.at[:, pl.ds(4 + a * own, own), pl.ds(0, rows)]
                else:
                    piece = source.at[:, pl.ds(4, own), pl.ds(rows - 8 if b == -1 else 0, 8)]
                    place = stage.at[0 if b == -1 else 1, :, pl.ds(4 + a * own, own)]
                copy = send(piece, place, partner)
                (near if abs(a) < 2 else later).append(copy)
        return near, later

    tile_row = iota((8, 128), 0)
    row256 = iota((8, 256), 0)

    def merged(stage, field, plane):
        return jnp.where(tile_row < 4, stage[1, field, plane], stage[0, field, plane])

    pl.semaphore_wait(barrier, len(partners))
    first = []
    for number, ref in enumerate((inx, iny, inz, src)):
        more = 3 if number == 0 else 2
        first.append(send(ref.at[pl.ds(8 - more, more)], IN.at[number, pl.ds(3 - more, more), pl.ds(0, 32)], (wide_at(1), j)))
        first.append(send(ref.at[pl.ds(0, 2)], IN.at[number, pl.ds(11, 2), pl.ds(0, 32)], (wide_at(-1), j)))

    for copy in loads:
        copy.wait()

    @pl.loop(0, 4)
    def pack(c):
        for p in (2 * c, 2 * c + 1):
            up = jnp.zeros((8, 256), F32)
            down = jnp.zeros((8, 256), F32)
            for f in range(4):
                mine = (row256 >> 1) == f
                up = jnp.where(mine, pltpu.roll(IN[f, 3 + p, 24:32], (2 * f + 2) % 8, 0), up)
                down = jnp.where(mine, pltpu.roll(IN[f, 3 + p, 0:8], 2 * f, 0), down)
            PKs[0, p] = up
            PKs[1, p] = down

    for p in range(8):
        FYs[p:p + 1] = IN[1, 3 + p, 29:30]

    for side, b in ((0, 1), (1, -1)):
        first.append(send(PKs.at[side], RK.at[side, pl.ds(2, 8)], (i, narrow_at(b))))
    first.append(send(FYs, FYr, (i, narrow_at(1))))
    for side, b in ((0, 1), (1, -1)):
        first.append(send(PKs.at[side, pl.ds(6, 2)], RK.at[side, pl.ds(0, 2)], (wide_at(1), narrow_at(b))))
        first.append(send(PKs.at[side, pl.ds(0, 2)], RK.at[side, pl.ds(10, 2)], (wide_at(-1), narrow_at(b))))

    pairs0 = ones_where((iota((256, 128), 0) >> 1) == iota((256, 128), 1))
    odds0 = ones_where(iota((256, 128), 0) == 2 * iota((256, 128), 1) + 1)
    pairs1 = ones_where((iota((128, 128), 0) >> 1) == iota((128, 128), 1))
    odds1 = ones_where(iota((128, 128), 0) == 2 * iota((128, 128), 1) + 1)
    pairs2 = ones_where((iota((128, 128), 0) >> 1) == (iota((128, 128), 1) & 31))
    odds2 = ones_where(iota((128, 128), 0) == 2 * (iota((128, 128), 1) & 31) + 1)

    def paired(tiles, odd_only=False):
        lanes = tiles[0].shape[1]
        half = tiles[0].shape[0] // 2
        for c, tile in enumerate(tiles):
            for part in range(lanes // 128):
                RZ[part, c, 0:2 * half] = tile[:, 128 * part:128 * (part + 1)]
        below = []
        for c in range(len(tiles)):
            beside = []
            for part in range(lanes // 128):
                odd = RZ[part, c, pl.ds(1, half, stride=2), :]
                beside.append(odd if odd_only else RZ[part, c, pl.ds(0, half, stride=2), :] + odd)
            below.append(jnp.concatenate(beside, axis=1) if len(beside) > 1 else beside[0])
        return jnp.concatenate(below, axis=0)

    def coarse_faces(f, at, target, own, rows, pairs, odds):
        half = rows // 2
        x = [f[0, at + 2 * c + 1, 0:rows] for c in range(own)]
        y = [f[1, at + 2 * c, 0:rows] + f[1, at + 2 * c + 1, 0:rows] for c in range(own)]
        z = [f[2, at + 2 * c, 0:rows] + f[2, at + 2 * c + 1, 0:rows] for c in range(own)]
        for number, (tiles, odd_only, chosen) in enumerate(((x, False, pairs), (y, True, pairs), (z, False, odds))):
            got = picked(paired(tiles, odd_only), chosen)
            for c in range(own):
                target[number, 4 + c, 0:half] = got[c * half:(c + 1) * half]

    coarse_faces(IN, 3, F1, 4, 32, pairs0, odds0)
    faces1, _ = exchange(F1, F1, F1S, 4, 16, 1)
    coarse_faces(F1, 4, F2, 2, 16, pairs1, odds1)
    near, later = exchange(F2, F2, F2S, 2, 8, 2)
    faces2 = near + later

    lane_block = iota((8, 128), 1) >> 5
    both_rows = (tile_row >> 1) == lane_block
    odd_rows = tile_row == 2 * lane_block + 1

    def to_row(tile, chosen, mask):
        got = jnp.where(mask, picked(tile, chosen), 0.0)
        return jnp.broadcast_to(jnp.sum(got, axis=0, keepdims=True), (narrow, 128))

    T3s[0] = to_row(F2[0, 5, 0:8], pairs2, both_rows)
    T3s[1] = to_row(F2[1, 4, 0:8] + F2[1, 5, 0:8], pairs2, odd_rows)
    T3s[2] = to_row(F2[2, 4, 0:8] + F2[2, 5, 0:8], odds2, both_rows)
    gather_f = [send(T3s, T3r.at[j], (i, narrow_at(d))) for d in range(1, narrow)]
    T3r[j] = T3s[...]

    arrive(first)
    has_low, has_high = j > 0, j < narrow - 1

    @pl.loop(0, 12)
    def unpack(q):
        low, high = RK[0, q], RK[1, q]
        for f in range(4):
            from_high = pltpu.roll(high, (8 - 2 * f) % 8, 0)
            from_low = pltpu.roll(low, (14 - 2 * f) % 8, 0)
            if f == 1:
                from_low = jnp.where(has_low, from_low, 0.0)
            IN[f, q + 1, 32:40] = jnp.where(row256 < 2, from_high, jnp.where(row256 >= 6, from_low, 0.0))

    IN[0, 0, 32:40] = jnp.zeros((8, 256), F32)
    for p in range(8):
        IN[1, 3 + p, 37:38] = jnp.where(has_low, FYr[p:p + 1], 0.0)

    @pl.when(i == 0)
    def _():
        IN[0, 2] = jnp.zeros((40, 256), F32)

    def inside(rows, lanes, own_rows, reach):
        row = iota((rows, lanes), 0)
        mask = (row < own_rows) | ((row < own_rows + reach) & has_high) | ((row >= rows - reach) & has_low)
        return mask

    def plane_in(p, own):
        return (i * own + p >= 0) & (i * own + p < own * wide)

    rows_in0 = inside(40, 256, 32, 2)
    weight_in = jnp.where(rows_in0, relax, 0.0)

    @pl.loop(-1, 5)
    def start0(c):
        p = 2 * c
        w = jnp.where(plane_in(p, 8), weight_in, 0.0)[None] / diagonal(IN, p + 3, 2)
        W0[pl.ds(p + 3, 2)] = w
        VA[pl.ds(p + 3, 2)] = w * IN[3, pl.ds(p + 3, 2)]

    @pl.loop(0, 5)
    def down0(c):
        sweep(VD, VA, IN.at[3], IN, W0, 2 * c + 2, 2)

    background = []
    background.append(send(VD.at[pl.ds(8, 3), pl.ds(0, 32)], VB.at[pl.ds(0, 3)], (wide_at(1), j)))
    background.append(send(VD.at[pl.ds(3, 3), pl.ds(0, 32)], VB.at[pl.ds(3, 3)], (wide_at(-1), j)))
    for side, b, row in ((0, 1, 24), (1, -1, 0)):
        background.append(send(VD.at[pl.ds(3, 8), pl.ds(row, 8)], VY.at[side, pl.ds(3, 8)], (i, narrow_at(b))))
        background.append(send(VD.at[pl.ds(8, 3), pl.ds(row, 8)], VY.at[side, pl.ds(0, 3)], (wide_at(1), narrow_at(b))))
        background.append(send(VD.at[pl.ds(3, 3), pl.ds(row, 8)], VY.at[side, pl.ds(11, 3)], (wide_at(-1), narrow_at(b))))

    @pl.loop(0, 4)
    def restrict0(c):
        both = remainder(IN.at[3], IN, VD, 2 * c + 3, 2)
        VE[c, 0:32] = both[0, :32] + both[1, :32]

    got = paired([VE[c, 0:32] for c in range(4)])
    got = picked(got, pairs0)
    for c in range(4):
        B1[0, 4 + c, 0:16] = got[16 * c:16 * (c + 1)]
    rhs1, _ = exchange(B1, B1, B1S, 4, 16, 1)

    arrive(gather_f)
    sub = iota((narrow, 128), 0)

    def assembled(parts):
        tile = parts[0]
        for n in range(1, narrow):
            tile = jnp.where(sub == n, parts[n], tile)
        return tile

    for f in range(3):
        G3f[f, zi, ri] = assembled([T3r[n, f] for n in range(narrow)])
    gather_f = [send(G3f.at[:, zi, ri], G3f.at[:, zi, ri], (lax.rem(zi + d, ring) * group + ri, j)) for d in range(1, ring)]

    def finish_faces(f, stage, planes, rows):
        for field in range(3):
            tile = jnp.where(tile_row[None] < 4, stage[1, field], stage[0, field])
            if field == 1:
                tile = jnp.where(((tile_row < 4) | has_low)[None], tile, 0.0)
            f[field, :, rows:rows + 8] = tile

        @pl.when(i == 0)
        def _():
            f[0, 3] = jnp.zeros(f.shape[2:], F32)

        if planes == 10:
            @pl.when(i == 1)
            def _():
                f[0, 1] = jnp.zeros(f.shape[2:], F32)

    arrive(faces1)
    finish_faces(F1, F1S, 12, 16)
    rows_in1 = inside(24, 128, 16, 4)
    weight_in1 = jnp.where(rows_in1, relax, 0.0)

    for p, n in ((-3, 3), (0, 4), (4, 4)):
        W1[p + 4:p + 4 + n] = jnp.where(plane_in(p, 4), weight_in1, 0.0)[None] / diagonal(F1, p + 4, n)

    arrive(rhs1)
    B1[0, :, 16:24] = jnp.where(tile_row[None] < 4, B1S[1, 0], B1S[0, 0])
    X1[2:10] = W1[2:10] * B1[0, 2:10]
    for p in (-1, 2):
        sweep(Y1.at[0], X1, B1.at[0], F1, W1, p + 4, 3)

    back1, _ = exchange(Y1, Y1R, Y1S, 4, 16, 1)
    rest = remainder(B1.at[0], F1, Y1.at[0], 4, 4)
    got = paired([rest[2 * c, :16] + rest[2 * c + 1, :16] for c in range(2)])
    got = picked(got, pairs1)
    for c in range(2):
        B2[0, 4 + c, 0:8] = got[8 * c:8 * (c + 1)]
    rhs2, rhs2_far = exchange(B2, B2, B2S, 2, 8, 2)

    arrive(gather_f)
    gather_f = [send(G3f.at[:, :, ri], G3f.at[:, :, ri], (zi * group + lax.rem(ri + d, group), j)) for d in range(1, group)]

    arrive(faces2)
    finish_faces(F2, F2S, 10, 8)
    rows_in2 = inside(16, 128, 8, 4) & (iota((16, 128), 1) < 64)

    weights = relax / diagonal(F2, 1, 9)
    for p in range(-3, 6):
        W2[p + 4] = jnp.where(rows_in2 & plane_in(p, 2), weights[p + 3], 0.0)

    arrive(rhs2)
    B2[0, 2:8, 8:16] = jnp.where(tile_row[None] < 4, B2S[1, 0, 2:8], B2S[0, 0, 2:8])
    X2[2:8] = W2[2:8] * B2[0, 2:8]
    sweep(Y2.at[0], X2, B2.at[0], F2, W2, 3, 4)
    back2_near, back2_far = exchange(Y2, Y2R, Y2S, 2, 8, 2)
    rest = remainder(B2.at[0], F2, Y2.at[0], 4, 2)
    B3s[...] = to_row(rest[0, :8] + rest[1, :8], pairs2, both_rows)
    gather_b = [send(B3s, B3r.at[j], (i, narrow_at(d))) for d in range(1, narrow)]
    B3r[j] = B3s[...]
    arrive(gather_b)
    G3b[zi, ri] = assembled([B3r[n] for n in range(narrow)])
    gather_b = [send(G3b.at[zi, ri], G3b.at[zi, ri], (lax.rem(zi + d, ring) * group + ri, j)) for d in range(1, ring)]

    arrive(gather_f)
    block3 = iota((narrow, 128), 1) >> 5
    lane3 = iota((narrow, 128), 1) & 31
    last_y = (sub == narrow - 1) & (block3 == 3)
    last_lane = lane3 == 31

    XG[0] = jnp.zeros((narrow, 128), F32)

    @pl.loop(0, ring)
    def masks3(a):
        y, z = G3f[1, a], G3f[2, a]
        planes = pl.ds(a * group, group)
        XG[pl.ds(a * group + 1, group)] = G3f[0, a]
        EG[planes] = jnp.where(last_y[None], y, 0.0) + jnp.where(last_lane[None], z, 0.0)
        YG[planes] = jnp.where(last_y[None], 0.0, y)
        ZG[planes] = jnp.where(last_lane[None], 0.0, z)

    arrive(gather_b)
    gather_b = [send(G3b.at[:, ri], G3b.at[:, ri], (zi * group + lax.rem(ri + d, group), j)) for d in range(1, group)]
    for p in (0, 1, wide + 2, wide + 3):
        PD[p] = jnp.zeros((narrow, 128), F32)
    for p in range(5):
        XS[p] = jnp.zeros((narrow, 128), F32)
    arrive(gather_b)

    def next_y3(cells):
        moved = pltpu.roll(cells, 96, 2)
        return jnp.where(block3[None] == 3, pltpu.roll(moved, narrow - 1, 1), moved)

    def last_y3(cells):
        moved = pltpu.roll(cells, 32, 2)
        return jnp.where(block3[None] == 0, pltpu.roll(moved, 1, 1), moved)

    def summed(total):
        return jnp.sum(jnp.sum(total, axis=0, keepdims=True), axis=1, keepdims=True)

    zero3 = jnp.zeros((narrow, 128), F32)
    total = zero3
    for a in range(ring):
        r = G3b[a]
        PD[2 + a * group:2 + (a + 1) * group] = r
        RR[a * group:(a + 1) * group] = r
        total = total + jnp.sum(r * r, axis=0)
    norm_first = summed(total)

    def curvature(keep):
        total = zero3
        for a in range(ring):
            p = a * group
            here = PD[p + 2:p + 2 + group]
            high = XG[p + 1:p + 1 + group] * (here - PD[p + 3:p + 3 + group])
            low = XG[p:p + group] * (PD[p + 1:p + 1 + group] - here)
            along_y = YG[p:p + group] * (here - next_y3(here))
            along_z = ZG[p:p + group] * (here - pltpu.roll(here, 127, 2))
            q = (EG[p:p + group] * here + (high - low)) + (
                (along_y - last_y3(along_y)) + (along_z - pltpu.roll(along_z, 1, 2)))
            if keep:
                QQ[p:p + group] = q
            total = total + jnp.sum(here * q, axis=0)
        return summed(total)

    def iteration(counter, norm_now):
        alpha = norm_now / curvature(True)
        for p in range(5):
            XS[p] = XS[p] + alpha * PD[i + p]
        total = zero3
        for a in range(ring):
            planes = slice(a * group, (a + 1) * group)
            r = RR[planes] - alpha * QQ[planes]
            RR[planes] = r
            total = total + jnp.sum(r * r, axis=0)
        norm_next = summed(total)
        beta = norm_next / norm_now
        for a in range(ring):
            p = a * group
            PD[p + 2:p + 2 + group] = RR[p:p + group] + beta * PD[p + 2:p + 2 + group]
        return norm_next

    norm_now = lax.fori_loop(0, CGI - 1, iteration, norm_first)
    alpha = norm_now / curvature(False)
    for p in range(5):
        XS[p] = XS[p] + alpha * PD[i + p]

    row16 = iota((16, 128), 0)
    wanted = ((row16 & 7) >> 1) == (iota((16, 128), 1) >> 5)
    spread2 = ones_where(((iota((128, 128), 1) >> 1) == (iota((128, 128), 0) & 31)) & (iota((128, 128), 1) < 64))
    high_j, low_j = jnp.minimum(j + 1, narrow - 1), jnp.maximum(j - 1, 0)
    spread = []
    for p in range(5):
        middle = jnp.broadcast_to(XS[p, pl.ds(j, 1), :], (16, 128))
        above = jnp.broadcast_to(XS[p, pl.ds(high_j, 1), :], (16, 128))
        below = jnp.broadcast_to(XS[p, pl.ds(low_j, 1), :], (16, 128))
        x = jnp.where(row16 < 8, middle, jnp.where(row16 < 12, above, below))
        spread.append(jnp.where(wanted, x, 0.0))
    spread = picked(jnp.concatenate(spread, axis=0), spread2)
    arrive(rhs2_far + back2_near + back2_far)
    reach2 = inside(16, 128, 8, 4)
    for p in (0, 1, 8, 9):
        B2[0, p, 8:16] = merged(B2S, 0, p)
    for p in range(-4, 6):
        own = Y2[0, p + 4, 0:8] if 0 <= p < 2 else Y2R[0, p + 4, 0:8]
        x = jnp.concatenate([own, merged(Y2S, 0, p + 4)], axis=0)
        c = (p + 4) // 2
        x = x + spread[16 * c:16 * (c + 1)]
        X2[p + 4] = jnp.where(reach2 & plane_in(p, 2), x, 0.0)
    sweep(Z2, X2, B2.at[0], F2, W2, 1, 8)
    sweep(X2, Z2, B2.at[0], F2, W2, 2, 6)

    spread1 = ones_where((iota((128, 128), 1) >> 1) == iota((128, 128), 0))
    spread = picked(jnp.concatenate([X2[p + 4] for p in range(-2, 4)], axis=0), spread1)
    for c in range(6):
        U1[c, pl.ds(0, 16, stride=2), :] = spread[16 * c:16 * (c + 1)]
        U1[c, pl.ds(1, 16, stride=2), :] = spread[16 * c:16 * (c + 1)]
    arrive(back1)
    reach1 = inside(24, 128, 16, 4)
    for p in range(-4, 8):
        c = (p + 4) // 2
        own = Y1[0, p + 4, 0:16] if 0 <= p < 4 else Y1R[0, p + 4, 0:16]
        edge = merged(Y1S, 0, p + 4) + jnp.where(tile_row < 4, U1[c, 16:24], U1[c, 24:32])
        x = jnp.concatenate([own + U1[c, 0:16], edge], axis=0)
        X1[p + 4] = jnp.where(reach1 & plane_in(p, 4), x, 0.0)

    for p in (-3, 2):
        sweep(Z1, X1, B1.at[0], F1, W1, p + 4, 5)
    for p in (-2, 2):
        sweep(X1, Z1, B1.at[0], F1, W1, p + 4, 4)

    spread0 = ones_where((iota((128, 256), 1) >> 1) == iota((128, 256), 0))
    spread = picked(jnp.concatenate([X1[p + 4] for p in range(-2, 6)], axis=0), spread0)
    for c in range(8):
        for half in (0, 128):
            part = spread[24 * c:24 * (c + 1), half:half + 128]
            U0[half // 128, c, pl.ds(0, 24, stride=2), :] = part
            U0[half // 128, c, pl.ds(1, 24, stride=2), :] = part
    arrive(background)
    reach0 = inside(40, 256, 32, 4)

    def corrected(p, own):
        c = lax.div(p + 4, 2)
        u = jnp.concatenate([U0[0, c], U0[1, c]], axis=1)
        edge = jnp.where(row256 < 4, VY[1, p + 3] + u[32:40], VY[0, p + 3] + u[40:48])
        x = jnp.concatenate([own + u[0:32], edge], axis=0)
        return jnp.where(reach0 & plane_in(p, 8), x, 0.0)

    @pl.loop(0, 8)
    def correct0(p):
        VE[p + 3] = corrected(p, VD[p + 3, 0:32])

    @pl.loop(0, 3)
    def correct0_ends(p):
        VE[p] = corrected(p - 3, VB[p])
        VE[p + 11] = corrected(p + 8, VB[p + 3])

    @pl.loop(0, 6)
    def up0(c):
        sweep(VA, VE, IN.at[3], IN, W0, 2 * c + 1, 2)

    @pl.loop(0, 5)
    def up0_again(c):
        sweep(VF, VA, IN.at[3], IN, W0, 2 * c + 2, 2)

    store = pltpu.make_async_copy(VF.at[pl.ds(3, 8), pl.ds(0, 32)], out_p, store_sem.at[0])
    store.start()

    @pl.loop(0, 4)
    def rest0(c):
        VE[pl.ds(2 * c, 2)] = remainder(IN.at[3], IN, VF, 2 * c + 3, 2)

    store_r = pltpu.make_async_copy(VE.at[pl.ds(0, 8), pl.ds(0, 32)], out_r, store_sem.at[1])
    store_r.start()
    for copy in sent:
        copy.wait_send()
    store.wait()
    store_r.wait()


def shards(sizes, source, face_x, face_y, face_z):
    wide, narrow, ring, group = sizes
    shape = jax.ShapeDtypeStruct((8, 32, 256), F32)

    def V(*size):
        return pltpu.VMEM(size, F32)

    scratch = [
        V(4, 13, 40, 256), V(2, 8, 8, 256), V(8, 256), V(8, 256), V(2, 12, 8, 256),
        V(14, 40, 256), V(14, 40, 256), V(14, 40, 256), V(6, 32, 256), V(2, 14, 8, 256), V(14, 40, 256), V(14, 40, 256),
        V(2, 4, 32, 128), V(2, 8, 48, 128),
        V(3, 12, 24, 128), V(2, 3, 12, 8, 128), V(1, 12, 24, 128), V(2, 1, 12, 8, 128), V(12, 24, 128), V(12, 24, 128),
        V(1, 12, 24, 128), V(1, 12, 24, 128), V(2, 1, 12, 8, 128), V(12, 24, 128), V(6, 32, 128),
        V(3, 10, 16, 128), V(2, 3, 10, 8, 128), V(1, 10, 16, 128), V(2, 1, 10, 8, 128), V(10, 16, 128), V(10, 16, 128),
        V(1, 10, 16, 128), V(1, 10, 16, 128), V(2, 1, 10, 8, 128), V(10, 16, 128),
        V(3, narrow, 128), V(narrow, 3, narrow, 128), V(3, ring, group, narrow, 128),
        V(narrow, 128), V(narrow, narrow, 128), V(ring, group, narrow, 128), V(wide, narrow, 128),
        V(wide + 1, narrow, 128), V(wide, narrow, 128), V(wide, narrow, 128),
        V(wide + 4, narrow, 128), V(wide, narrow, 128), V(wide, narrow, 128), V(5, narrow, 128),
        pltpu.SemaphoreType.DMA((144,)), pltpu.SemaphoreType.DMA((144,)), pltpu.SemaphoreType.DMA((4,)),
        pltpu.SemaphoreType.DMA((2,)),
    ]
    anywhere = pl.BlockSpec(memory_space=pl.ANY)
    return pl.pallas_call(
        functools.partial(body, sizes),
        out_shape=(shape, shape),
        in_specs=[anywhere] * 4,
        out_specs=(anywhere, anywhere),
        scratch_shapes=scratch,
        compiler_params=pltpu.CompilerParams(collective_id=0, has_side_effects=True, vmem_limit_bytes=60 * 1024 * 1024),
    )(source, face_x, face_y, face_z)


def solution(mesh):
    wide, narrow = mesh.shape["wide"], mesh.shape["narrow"]
    group = 8 if wide == 64 else wide // 2
    spec = P("wide", "narrow", None)
    return jax.shard_map(
        functools.partial(shards, (wide, narrow, wide // group, group)),
        mesh=mesh,
        in_specs=(spec,) * 4,
        out_specs=(spec, spec),
        check_vma=False,
    )
```

```python
import functools

import jax
import jax.numpy as jnp
from jax import lax
from jax.experimental import pallas as pl
from jax.experimental.pallas import tpu as pltpu
from jax.sharding import PartitionSpec as P

CGI = 6
relax = 0.8
MESH = pl.DeviceIdType.MESH
F32 = jnp.float32
BF16 = jnp.bfloat16


def iota(shape, dim):
    return lax.broadcasted_iota(jnp.int32, shape, dim)


def picked(values, chosen):
    high = values.astype(BF16)
    rest = values - high.astype(F32)
    middle = rest.astype(BF16)
    low = (rest - middle.astype(F32)).astype(BF16)
    product = functools.partial(jnp.dot, preferred_element_type=F32)
    return product(high, chosen) + product(middle, chosen) + product(low, chosen)


def ones_where(condition):
    return jnp.where(condition, 1.0, 0.0).astype(BF16)


def next_z(cells):
    lanes = cells.shape[-1]
    lane = iota(cells.shape[:-1] + (128,), len(cells.shape) - 1)
    axis = len(cells.shape) - 1
    if lanes == 128:
        return jnp.where(lane == 127, 0.0, pltpu.roll(cells, 127, axis))
    first = pltpu.roll(cells[..., :128], 127, axis)
    second = pltpu.roll(cells[..., 128:], 127, axis)
    return jnp.concatenate([jnp.where(lane == 127, second, first), jnp.where(lane == 127, 0.0, second)], axis=axis)


def last_z(cells):
    lanes = cells.shape[-1]
    lane = iota(cells.shape[:-1] + (128,), len(cells.shape) - 1)
    axis = len(cells.shape) - 1
    if lanes == 128:
        return jnp.where(lane == 0, 0.0, pltpu.roll(cells, 1, axis))
    first = pltpu.roll(cells[..., :128], 1, axis)
    second = pltpu.roll(cells[..., 128:], 1, axis)
    return jnp.concatenate([jnp.where(lane == 0, 0.0, first), jnp.where(lane == 0, first, second)], axis=axis)


def remainder(b, f, v, p, n=1):
    here = v[pl.ds(p, n)]
    rows = here.shape[1]
    flow = f[0, pl.ds(p, n)] * (v[pl.ds(p + 1, n)] - here) - f[0, pl.ds(p - 1, n)] * (here - v[pl.ds(p - 1, n)])
    along = f[1, pl.ds(p, n)] * (pltpu.roll(here, rows - 1, 1) - here)
    flow = flow + (along - pltpu.roll(along, 1, 1))
    along = f[2, pl.ds(p, n)] * (next_z(here) - here)
    flow = flow + (along - last_z(along))
    return b[pl.ds(p, n)] + flow


def diagonal(f, p, n=1):
    x, y, z = f[0, pl.ds(p, n)], f[1, pl.ds(p, n)], f[2, pl.ds(p, n)]
    return (x + f[0, pl.ds(p - 1, n)]) + (y + pltpu.roll(y, 1, 1)) + (z + last_z(z))


def sweep(target, v, b, f, w, p, n):
    target[pl.ds(p, n)] = v[pl.ds(p, n)] + w[pl.ds(p, n)] * remainder(b, f, v, p, n)


def body(sizes, src, inx, iny, inz, out_p, out_r, IN, PKs, FYs, FYr, RK, W0, VA, VD, VB, VY, VE, VF, RZ, U0,
         F1, F1S, B1, B1S, W1, X1, Y1, Y1R, Y1S, Z1, U1, F2, F2S, B2, B2S, W2, X2, Y2, Y2R, Y2S, Z2,
         T3s, T3r, G3f, B3s, B3r, G3b, EG, XG, YG, ZG, PD, RR, QQ, XS, send_sem, recv_sem, load_sem, store_sem):
    wide, narrow, ring, group = sizes
    i, j = lax.axis_index("wide"), lax.axis_index("narrow")
    zi, ri = lax.div(i, group), lax.rem(i, group)

    def wide_at(step):
        return lax.rem(i + (step + wide), wide)

    def narrow_at(step):
        return lax.rem(j + (step + narrow), narrow)

    loads = []
    for number, ref in enumerate((inx, iny, inz, src)):
        loads.append(pltpu.make_async_copy(ref, IN.at[number, pl.ds(3, 8), pl.ds(0, 32)], load_sem.at[number]))
        loads[-1].start()

    barrier = pltpu.get_barrier_semaphore()
    partners = [(wide_at(a), narrow_at(b)) for a in (0, 1, -1, 2, -2) for b in (0, 1, -1) if (a, b) != (0, 0)]
    partners += [(i, narrow_at(d)) for d in range(2, narrow - 1)]
    partners += [(lax.rem(zi + d, ring) * group + ri, j) for d in range(1, ring)]
    partners += [(zi * group + lax.rem(ri + d, group), j) for d in range(1, group)]
    for partner in partners:
        pl.semaphore_signal(barrier, inc=1, device_id=partner, device_id_type=MESH)

    sent = []

    def send(source, target, partner):
        number = len(sent)
        copy = pltpu.make_async_remote_copy(
            src_ref=source, dst_ref=target, send_sem=send_sem.at[number], recv_sem=recv_sem.at[number],
            device_id=partner, device_id_type=MESH)
        copy.start()
        sent.append(copy)
        return copy

    def arrive(copies):
        for copy in copies:
            copy.wait_recv()

    def exchange(source, target, stage, own, rows, steps):
        copies = []
        for a in steps:
            for b in (0, 1, -1):
                if (a, b) == (0, 0):
                    continue
                partner = (wide_at(-a), narrow_at(-b))
                if b == 0:
                    piece = source.at[:, pl.ds(4, own), pl.ds(0, rows)]
                    place = target.at[:, pl.ds(4 + a * own, own), pl.ds(0, rows)]
                else:
                    piece = source.at[:, pl.ds(4, own), pl.ds(rows - 8 if b == -1 else 0, 8)]
                    place = stage.at[0 if b == -1 else 1, :, pl.ds(4 + a * own, own)]
                copies.append(send(piece, place, partner))
        return copies

    near, far = (0, 1, -1), (2, -2)

    tile_row = iota((8, 128), 0)
    row256 = iota((8, 256), 0)

    def merged(stage, field, plane):
        return jnp.where(tile_row < 4, stage[1, field, plane], stage[0, field, plane])

    pl.semaphore_wait(barrier, len(partners))
    first = []
    for number, ref in enumerate((inx, iny, inz, src)):
        more = 3 if number == 0 else 2
        first.append(send(ref.at[pl.ds(8 - more, more)], IN.at[number, pl.ds(3 - more, more), pl.ds(0, 32)], (wide_at(1), j)))
        first.append(send(ref.at[pl.ds(0, 2)], IN.at[number, pl.ds(11, 2), pl.ds(0, 32)], (wide_at(-1), j)))

    for copy in loads:
        copy.wait()

    @pl.loop(0, 4)
    def pack(c):
        for p in (2 * c, 2 * c + 1):
            up = jnp.zeros((8, 256), F32)
            down = jnp.zeros((8, 256), F32)
            for f in range(4):
                mine = (row256 >> 1) == f
                up = jnp.where(mine, pltpu.roll(IN[f, 3 + p, 24:32], (2 * f + 2) % 8, 0), up)
                down = jnp.where(mine, pltpu.roll(IN[f, 3 + p, 0:8], 2 * f, 0), down)
            PKs[0, p] = up
            PKs[1, p] = down

    for p in range(8):
        FYs[p:p + 1] = IN[1, 3 + p, 29:30]

    for side, b in ((0, 1), (1, -1)):
        first.append(send(PKs.at[side], RK.at[side, pl.ds(2, 8)], (i, narrow_at(b))))
    first.append(send(FYs, FYr, (i, narrow_at(1))))
    for side, b in ((0, 1), (1, -1)):
        first.append(send(PKs.at[side, pl.ds(6, 2)], RK.at[side, pl.ds(0, 2)], (wide_at(1), narrow_at(b))))
        first.append(send(PKs.at[side, pl.ds(0, 2)], RK.at[side, pl.ds(10, 2)], (wide_at(-1), narrow_at(b))))

    pairs0 = ones_where((iota((256, 128), 0) >> 1) == iota((256, 128), 1))
    odds0 = ones_where(iota((256, 128), 0) == 2 * iota((256, 128), 1) + 1)
    pairs1 = ones_where((iota((128, 128), 0) >> 1) == iota((128, 128), 1))
    odds1 = ones_where(iota((128, 128), 0) == 2 * iota((128, 128), 1) + 1)
    pairs2 = ones_where((iota((128, 128), 0) >> 1) == (iota((128, 128), 1) & 31))
    odds2 = ones_where(iota((128, 128), 0) == 2 * (iota((128, 128), 1) & 31) + 1)

    def paired(tiles, odd_only=False):
        lanes = tiles[0].shape[1]
        half = tiles[0].shape[0] // 2
        for c, tile in enumerate(tiles):
            for part in range(lanes // 128):
                RZ[part, c, 0:2 * half] = tile[:, 128 * part:128 * (part + 1)]
        below = []
        for c in range(len(tiles)):
            beside = []
            for part in range(lanes // 128):
                odd = RZ[part, c, pl.ds(1, half, stride=2), :]
                beside.append(odd if odd_only else RZ[part, c, pl.ds(0, half, stride=2), :] + odd)
            below.append(jnp.concatenate(beside, axis=1) if len(beside) > 1 else beside[0])
        return jnp.concatenate(below, axis=0)

    def coarse_faces(f, at, target, own, rows, pairs, odds):
        half = rows // 2
        x = [f[0, at + 2 * c + 1, 0:rows] for c in range(own)]
        y = [f[1, at + 2 * c, 0:rows] + f[1, at + 2 * c + 1, 0:rows] for c in range(own)]
        z = [f[2, at + 2 * c, 0:rows] + f[2, at + 2 * c + 1, 0:rows] for c in range(own)]
        for number, (tiles, odd_only, chosen) in enumerate(((x, False, pairs), (y, True, pairs), (z, False, odds))):
            got = picked(paired(tiles, odd_only), chosen)
            for c in range(own):
                target[number, 4 + c, 0:half] = got[c * half:(c + 1) * half]

    coarse_faces(IN, 3, F1, 4, 32, pairs0, odds0)
    faces1 = exchange(F1, F1, F1S, 4, 16, near)
    coarse_faces(F1, 4, F2, 2, 16, pairs1, odds1)

    lane_block = iota((8, 128), 1) >> 5
    both_rows = (tile_row >> 1) == lane_block
    odd_rows = tile_row == 2 * lane_block + 1

    def to_row(tile, chosen, mask):
        got = jnp.where(mask, picked(tile, chosen), 0.0)
        return jnp.broadcast_to(jnp.sum(got, axis=0, keepdims=True), (narrow, 128))

    T3s[0] = to_row(F2[0, 5, 0:8], pairs2, both_rows)
    T3s[1] = to_row(F2[1, 4, 0:8] + F2[1, 5, 0:8], pairs2, odd_rows)
    T3s[2] = to_row(F2[2, 4, 0:8] + F2[2, 5, 0:8], odds2, both_rows)
    gather_f = [send(T3s, T3r.at[j], (i, narrow_at(d))) for d in range(1, narrow)]
    T3r[j] = T3s[...]

    arrive(first)
    has_low, has_high = j > 0, j < narrow - 1

    @pl.loop(0, 12)
    def unpack(q):
        low, high = RK[0, q], RK[1, q]
        for f in range(4):
            from_high = pltpu.roll(high, (8 - 2 * f) % 8, 0)
            from_low = pltpu.roll(low, (14 - 2 * f) % 8, 0)
            if f == 1:
                from_low = jnp.where(has_low, from_low, 0.0)
            IN[f, q + 1, 32:40] = jnp.where(row256 < 2, from_high, jnp.where(row256 >= 6, from_low, 0.0))

    IN[0, 0, 32:40] = jnp.zeros((8, 256), F32)
    for p in range(8):
        IN[1, 3 + p, 37:38] = jnp.where(has_low, FYr[p:p + 1], 0.0)

    @pl.when(i == 0)
    def _():
        IN[0, 2] = jnp.zeros((40, 256), F32)

    def inside(rows, lanes, own_rows, reach):
        row = iota((rows, lanes), 0)
        mask = (row < own_rows) | ((row < own_rows + reach) & has_high) | ((row >= rows - reach) & has_low)
        return mask

    def plane_in(p, own):
        return (i * own + p >= 0) & (i * own + p < own * wide)

    rows_in0 = inside(40, 256, 32, 2)
    weight_in = jnp.where(rows_in0, relax, 0.0)

    @pl.loop(-1, 5)
    def start0(c):
        p = 2 * c
        w = jnp.where(plane_in(p, 8), weight_in, 0.0)[None] / diagonal(IN, p + 3, 2)
        W0[pl.ds(p + 3, 2)] = w
        VA[pl.ds(p + 3, 2)] = w * IN[3, pl.ds(p + 3, 2)]

    @pl.loop(0, 5)
    def down0(c):
        sweep(VD, VA, IN.at[3], IN, W0, 2 * c + 2, 2)

    @pl.loop(0, 4)
    def restrict0(c):
        both = remainder(IN.at[3], IN, VD, 2 * c + 3, 2)
        VE[c, 0:32] = both[0, :32] + both[1, :32]

    got = paired([VE[c, 0:32] for c in range(4)])
    got = picked(got, pairs0)
    for c in range(4):
        B1[0, 4 + c, 0:16] = got[16 * c:16 * (c + 1)]
    rhs1 = exchange(B1, B1, B1S, 4, 16, near)
    faces2 = exchange(F2, F2, F2S, 2, 8, near + far)

    arrive(gather_f)
    sub = iota((narrow, 128), 0)

    def assembled(parts):
        tile = parts[0]
        for n in range(1, narrow):
            tile = jnp.where(sub == n, parts[n], tile)
        return tile

    for f in range(3):
        G3f[f, zi, ri] = assembled([T3r[n, f] for n in range(narrow)])
    gather_f = [send(G3f.at[:, zi, ri], G3f.at[:, zi, ri], (lax.rem(zi + d, ring) * group + ri, j)) for d in range(1, ring)]

    def finish_faces(f, stage, planes, rows):
        for field in range(3):
            tile = jnp.where(tile_row[None] < 4, stage[1, field], stage[0, field])
            if field == 1:
                tile = jnp.where(((tile_row < 4) | has_low)[None], tile, 0.0)
            f[field, :, rows:rows + 8] = tile

        @pl.when(i == 0)
        def _():
            f[0, 3] = jnp.zeros(f.shape[2:], F32)

        if planes == 10:
            @pl.when(i == 1)
            def _():
                f[0, 1] = jnp.zeros(f.shape[2:], F32)

    arrive(faces1)
    finish_faces(F1, F1S, 12, 16)
    rows_in1 = inside(24, 128, 16, 4)
    weight_in1 = jnp.where(rows_in1, relax, 0.0)

    for p, n in ((-3, 3), (0, 4), (4, 4)):
        W1[p + 4:p + 4 + n] = jnp.where(plane_in(p, 4), weight_in1, 0.0)[None] / diagonal(F1, p + 4, n)

    arrive(rhs1)
    B1[0, :, 16:24] = jnp.where(tile_row[None] < 4, B1S[1, 0], B1S[0, 0])
    X1[2:10] = W1[2:10] * B1[0, 2:10]
    for p in (-1, 2):
        sweep(Y1.at[0], X1, B1.at[0], F1, W1, p + 4, 3)

    rest = remainder(B1.at[0], F1, Y1.at[0], 4, 4)
    got = paired([rest[2 * c, :16] + rest[2 * c + 1, :16] for c in range(2)])
    got = picked(got, pairs1)
    for c in range(2):
        B2[0, 4 + c, 0:8] = got[8 * c:8 * (c + 1)]
    rhs2 = exchange(B2, B2, B2S, 2, 8, near)

    arrive(gather_f)
    gather_f = [send(G3f.at[:, :, ri], G3f.at[:, :, ri], (zi * group + lax.rem(ri + d, group), j)) for d in range(1, group)]

    arrive(faces2)
    finish_faces(F2, F2S, 10, 8)
    rows_in2 = inside(16, 128, 8, 4) & (iota((16, 128), 1) < 64)

    weights = relax / diagonal(F2, 1, 9)
    for p in range(-3, 6):
        W2[p + 4] = jnp.where(rows_in2 & plane_in(p, 2), weights[p + 3], 0.0)

    arrive(rhs2)
    B2[0, 2:8, 8:16] = jnp.where(tile_row[None] < 4, B2S[1, 0, 2:8], B2S[0, 0, 2:8])
    X2[2:8] = W2[2:8] * B2[0, 2:8]
    sweep(Y2.at[0], X2, B2.at[0], F2, W2, 3, 4)
    rest = remainder(B2.at[0], F2, Y2.at[0], 4, 2)
    B3s[...] = to_row(rest[0, :8] + rest[1, :8], pairs2, both_rows)
    gather_b = [send(B3s, B3r.at[j], (i, narrow_at(d))) for d in range(1, narrow)]
    B3r[j] = B3s[...]
    arrive(gather_b)
    G3b[zi, ri] = assembled([B3r[n] for n in range(narrow)])
    gather_b = [send(G3b.at[zi, ri], G3b.at[zi, ri], (lax.rem(zi + d, ring) * group + ri, j)) for d in range(1, ring)]

    arrive(gather_f)
    block3 = iota((narrow, 128), 1) >> 5
    lane3 = iota((narrow, 128), 1) & 31
    last_y = (sub == narrow - 1) & (block3 == 3)
    last_lane = lane3 == 31

    XG[0] = jnp.zeros((narrow, 128), F32)

    @pl.loop(0, ring)
    def masks3(a):
        y, z = G3f[1, a], G3f[2, a]
        planes = pl.ds(a * group, group)
        XG[pl.ds(a * group + 1, group)] = G3f[0, a]
        EG[planes] = jnp.where(last_y[None], y, 0.0) + jnp.where(last_lane[None], z, 0.0)
        YG[planes] = jnp.where(last_y[None], 0.0, y)
        ZG[planes] = jnp.where(last_lane[None], 0.0, z)

    arrive(gather_b)
    gather_b = [send(G3b.at[:, ri], G3b.at[:, ri], (zi * group + lax.rem(ri + d, group), j)) for d in range(1, group)]

    back2 = exchange(Y2, Y2R, Y2S, 2, 8, near + far) + exchange(B2, B2, B2S, 2, 8, far)
    back1 = exchange(Y1, Y1R, Y1S, 4, 16, near)
    background = []
    background.append(send(VD.at[pl.ds(8, 3), pl.ds(0, 32)], VB.at[pl.ds(0, 3)], (wide_at(1), j)))
    background.append(send(VD.at[pl.ds(3, 3), pl.ds(0, 32)], VB.at[pl.ds(3, 3)], (wide_at(-1), j)))
    for side, b, row in ((0, 1, 24), (1, -1, 0)):
        background.append(send(VD.at[pl.ds(3, 8), pl.ds(row, 8)], VY.at[side, pl.ds(3, 8)], (i, narrow_at(b))))
        background.append(send(VD.at[pl.ds(8, 3), pl.ds(row, 8)], VY.at[side, pl.ds(0, 3)], (wide_at(1), narrow_at(b))))
        background.append(send(VD.at[pl.ds(3, 3), pl.ds(row, 8)], VY.at[side, pl.ds(11, 3)], (wide_at(-1), narrow_at(b))))

    for p in (0, 1, wide + 2, wide + 3):
        PD[p] = jnp.zeros((narrow, 128), F32)
    for p in range(5):
        XS[p] = jnp.zeros((narrow, 128), F32)
    arrive(gather_b)

    def next_y3(cells):
        moved = pltpu.roll(cells, 96, 2)
        return jnp.where(block3[None] == 3, pltpu.roll(moved, narrow - 1, 1), moved)

    def last_y3(cells):
        moved = pltpu.roll(cells, 32, 2)
        return jnp.where(block3[None] == 0, pltpu.roll(moved, 1, 1), moved)

    def summed(total):
        return jnp.sum(jnp.sum(total, axis=0, keepdims=True), axis=1, keepdims=True)

    zero3 = jnp.zeros((narrow, 128), F32)
    total = zero3
    for a in range(ring):
        r = G3b[a]
        PD[2 + a * group:2 + (a + 1) * group] = r
        RR[a * group:(a + 1) * group] = r
        total = total + jnp.sum(r * r, axis=0)
    norm_first = summed(total)

    def curvature(keep):
        total = zero3
        for a in range(ring):
            p = a * group
            here = PD[p + 2:p + 2 + group]
            high = XG[p + 1:p + 1 + group] * (here - PD[p + 3:p + 3 + group])
            low = XG[p:p + group] * (PD[p + 1:p + 1 + group] - here)
            along_y = YG[p:p + group] * (here - next_y3(here))
            along_z = ZG[p:p + group] * (here - pltpu.roll(here, 127, 2))
            q = (EG[p:p + group] * here + (high - low)) + (
                (along_y - last_y3(along_y)) + (along_z - pltpu.roll(along_z, 1, 2)))
            if keep:
                QQ[p:p + group] = q
            total = total + jnp.sum(here * q, axis=0)
        return summed(total)

    def iteration(counter, norm_now):
        alpha = norm_now / curvature(True)
        for p in range(5):
            XS[p] = XS[p] + alpha * PD[i + p]
        total = zero3
        for a in range(ring):
            planes = slice(a * group, (a + 1) * group)
            r = RR[planes] - alpha * QQ[planes]
            RR[planes] = r
            total = total + jnp.sum(r * r, axis=0)
        norm_next = summed(total)
        beta = norm_next / norm_now
        for a in range(ring):
            p = a * group
            PD[p + 2:p + 2 + group] = RR[p:p + group] + beta * PD[p + 2:p + 2 + group]
        return norm_next

    norm_now = lax.fori_loop(0, CGI - 1, iteration, norm_first)
    alpha = norm_now / curvature(False)
    for p in range(5):
        XS[p] = XS[p] + alpha * PD[i + p]

    row16 = iota((16, 128), 0)
    wanted = ((row16 & 7) >> 1) == (iota((16, 128), 1) >> 5)
    spread2 = ones_where(((iota((128, 128), 1) >> 1) == (iota((128, 128), 0) & 31)) & (iota((128, 128), 1) < 64))
    high_j, low_j = jnp.minimum(j + 1, narrow - 1), jnp.maximum(j - 1, 0)
    spread = []
    for p in range(5):
        middle = jnp.broadcast_to(XS[p, pl.ds(j, 1), :], (16, 128))
        above = jnp.broadcast_to(XS[p, pl.ds(high_j, 1), :], (16, 128))
        below = jnp.broadcast_to(XS[p, pl.ds(low_j, 1), :], (16, 128))
        x = jnp.where(row16 < 8, middle, jnp.where(row16 < 12, above, below))
        spread.append(jnp.where(wanted, x, 0.0))
    spread = picked(jnp.concatenate(spread, axis=0), spread2)
    arrive(back2)
    reach2 = inside(16, 128, 8, 4)
    for p in (0, 1, 8, 9):
        B2[0, p, 8:16] = merged(B2S, 0, p)
    for p in range(-4, 6):
        own = Y2[0, p + 4, 0:8] if 0 <= p < 2 else Y2R[0, p + 4, 0:8]
        x = jnp.concatenate([own, merged(Y2S, 0, p + 4)], axis=0)
        c = (p + 4) // 2
        x = x + spread[16 * c:16 * (c + 1)]
        X2[p + 4] = jnp.where(reach2 & plane_in(p, 2), x, 0.0)
    sweep(Z2, X2, B2.at[0], F2, W2, 1, 8)
    sweep(X2, Z2, B2.at[0], F2, W2, 2, 6)

    spread1 = ones_where((iota((128, 128), 1) >> 1) == iota((128, 128), 0))
    spread = picked(jnp.concatenate([X2[p + 4] for p in range(-2, 4)], axis=0), spread1)
    for c in range(6):
        U1[c, pl.ds(0, 16, stride=2), :] = spread[16 * c:16 * (c + 1)]
        U1[c, pl.ds(1, 16, stride=2), :] = spread[16 * c:16 * (c + 1)]
    arrive(back1)
    reach1 = inside(24, 128, 16, 4)
    for p in range(-4, 8):
        c = (p + 4) // 2
        own = Y1[0, p + 4, 0:16] if 0 <= p < 4 else Y1R[0, p + 4, 0:16]
        edge = merged(Y1S, 0, p + 4) + jnp.where(tile_row < 4, U1[c, 16:24], U1[c, 24:32])
        x = jnp.concatenate([own + U1[c, 0:16], edge], axis=0)
        X1[p + 4] = jnp.where(reach1 & plane_in(p, 4), x, 0.0)

    for p in (-3, 2):
        sweep(Z1, X1, B1.at[0], F1, W1, p + 4, 5)
    for p in (-2, 2):
        sweep(X1, Z1, B1.at[0], F1, W1, p + 4, 4)

    spread0 = ones_where((iota((128, 256), 1) >> 1) == iota((128, 256), 0))
    spread = picked(jnp.concatenate([X1[p + 4] for p in range(-2, 6)], axis=0), spread0)
    for c in range(8):
        for half in (0, 128):
            part = spread[24 * c:24 * (c + 1), half:half + 128]
            U0[half // 128, c, pl.ds(0, 24, stride=2), :] = part
            U0[half // 128, c, pl.ds(1, 24, stride=2), :] = part
    arrive(background)
    reach0 = inside(40, 256, 32, 4)

    def corrected(p, own):
        c = lax.div(p + 4, 2)
        u = jnp.concatenate([U0[0, c], U0[1, c]], axis=1)
        edge = jnp.where(row256 < 4, VY[1, p + 3] + u[32:40], VY[0, p + 3] + u[40:48])
        x = jnp.concatenate([own + u[0:32], edge], axis=0)
        return jnp.where(reach0 & plane_in(p, 8), x, 0.0)

    @pl.loop(0, 8)
    def correct0(p):
        VE[p + 3] = corrected(p, VD[p + 3, 0:32])

    @pl.loop(0, 3)
    def correct0_ends(p):
        VE[p] = corrected(p - 3, VB[p])
        VE[p + 11] = corrected(p + 8, VB[p + 3])

    @pl.loop(0, 6)
    def up0(c):
        sweep(VA, VE, IN.at[3], IN, W0, 2 * c + 1, 2)

    @pl.loop(0, 5)
    def up0_again(c):
        sweep(VF, VA, IN.at[3], IN, W0, 2 * c + 2, 2)

    store = pltpu.make_async_copy(VF.at[pl.ds(3, 8), pl.ds(0, 32)], out_p, store_sem.at[0])
    store.start()

    @pl.loop(0, 4)
    def rest0(c):
        VE[pl.ds(2 * c, 2)] = remainder(IN.at[3], IN, VF, 2 * c + 3, 2)

    store_r = pltpu.make_async_copy(VE.at[pl.ds(0, 8), pl.ds(0, 32)], out_r, store_sem.at[1])
    store_r.start()
    for copy in sent:
        copy.wait_send()
    store.wait()
    store_r.wait()


def shards(sizes, source, face_x, face_y, face_z):
    wide, narrow, ring, group = sizes
    shape = jax.ShapeDtypeStruct((8, 32, 256), F32)

    def V(*size):
        return pltpu.VMEM(size, F32)

    scratch = [
        V(4, 13, 40, 256), V(2, 8, 8, 256), V(8, 256), V(8, 256), V(2, 12, 8, 256),
        V(14, 40, 256), V(14, 40, 256), V(14, 40, 256), V(6, 32, 256), V(2, 14, 8, 256), V(14, 40, 256), V(14, 40, 256),
        V(2, 4, 32, 128), V(2, 8, 48, 128),
        V(3, 12, 24, 128), V(2, 3, 12, 8, 128), V(1, 12, 24, 128), V(2, 1, 12, 8, 128), V(12, 24, 128), V(12, 24, 128),
        V(1, 12, 24, 128), V(1, 12, 24, 128), V(2, 1, 12, 8, 128), V(12, 24, 128), V(6, 32, 128),
        V(3, 10, 16, 128), V(2, 3, 10, 8, 128), V(1, 10, 16, 128), V(2, 1, 10, 8, 128), V(10, 16, 128), V(10, 16, 128),
        V(1, 10, 16, 128), V(1, 10, 16, 128), V(2, 1, 10, 8, 128), V(10, 16, 128),
        V(3, narrow, 128), V(narrow, 3, narrow, 128), V(3, ring, group, narrow, 128),
        V(narrow, 128), V(narrow, narrow, 128), V(ring, group, narrow, 128), V(wide, narrow, 128),
        V(wide + 1, narrow, 128), V(wide, narrow, 128), V(wide, narrow, 128),
        V(wide + 4, narrow, 128), V(wide, narrow, 128), V(wide, narrow, 128), V(5, narrow, 128),
        pltpu.SemaphoreType.DMA((144,)), pltpu.SemaphoreType.DMA((144,)), pltpu.SemaphoreType.DMA((4,)),
        pltpu.SemaphoreType.DMA((2,)),
    ]
    anywhere = pl.BlockSpec(memory_space=pl.ANY)
    return pl.pallas_call(
        functools.partial(body, sizes),
        out_shape=(shape, shape),
        in_specs=[anywhere] * 4,
        out_specs=(anywhere, anywhere),
        scratch_shapes=scratch,
        compiler_params=pltpu.CompilerParams(collective_id=0, has_side_effects=True, vmem_limit_bytes=60 * 1024 * 1024),
    )(source, face_x, face_y, face_z)


def solution(mesh):
    wide, narrow = mesh.shape["wide"], mesh.shape["narrow"]
    group = 8 if wide == 64 else wide // 2
    spec = P("wide", "narrow", None)
    return jax.shard_map(
        functools.partial(shards, (wide, narrow, wide // group, group)),
        mesh=mesh,
        in_specs=(spec,) * 4,
        out_specs=(spec, spec),
        check_vma=False,
    )
```

```python
import functools

import jax
import jax.numpy as jnp
from jax import lax
from jax.experimental import pallas as pl
from jax.experimental.pallas import tpu as pltpu
from jax.sharding import PartitionSpec as P

CGI = 6
relax = 0.8
MESH = pl.DeviceIdType.MESH
F32 = jnp.float32
BF16 = jnp.bfloat16


def iota(shape, dim):
    return lax.broadcasted_iota(jnp.int32, shape, dim)


def picked(values, chosen):
    high = values.astype(BF16)
    rest = values - high.astype(F32)
    middle = rest.astype(BF16)
    low = (rest - middle.astype(F32)).astype(BF16)
    product = functools.partial(jnp.dot, preferred_element_type=F32)
    return product(high, chosen) + product(middle, chosen) + product(low, chosen)


def ones_where(condition):
    return jnp.where(condition, 1.0, 0.0).astype(BF16)


def next_z(cells):
    lanes = cells.shape[-1]
    lane = iota(cells.shape[:-1] + (128,), len(cells.shape) - 1)
    axis = len(cells.shape) - 1
    if lanes == 128:
        return jnp.where(lane == 127, 0.0, pltpu.roll(cells, 127, axis))
    first = pltpu.roll(cells[..., :128], 127, axis)
    second = pltpu.roll(cells[..., 128:], 127, axis)
    return jnp.concatenate([jnp.where(lane == 127, second, first), jnp.where(lane == 127, 0.0, second)], axis=axis)


def last_z(cells):
    lanes = cells.shape[-1]
    lane = iota(cells.shape[:-1] + (128,), len(cells.shape) - 1)
    axis = len(cells.shape) - 1
    if lanes == 128:
        return jnp.where(lane == 0, 0.0, pltpu.roll(cells, 1, axis))
    first = pltpu.roll(cells[..., :128], 1, axis)
    second = pltpu.roll(cells[..., 128:], 1, axis)
    return jnp.concatenate([jnp.where(lane == 0, 0.0, first), jnp.where(lane == 0, first, second)], axis=axis)


def remainder(b, f, v, p, n=1):
    here = v[pl.ds(p, n)]
    rows = here.shape[1]
    flow = f[0, pl.ds(p, n)] * (v[pl.ds(p + 1, n)] - here) - f[0, pl.ds(p - 1, n)] * (here - v[pl.ds(p - 1, n)])
    along = f[1, pl.ds(p, n)] * (pltpu.roll(here, rows - 1, 1) - here)
    flow = flow + (along - pltpu.roll(along, 1, 1))
    along = f[2, pl.ds(p, n)] * (next_z(here) - here)
    flow = flow + (along - last_z(along))
    return b[pl.ds(p, n)] + flow


def diagonal(f, p, n=1):
    x, y, z = f[0, pl.ds(p, n)], f[1, pl.ds(p, n)], f[2, pl.ds(p, n)]
    return (x + f[0, pl.ds(p - 1, n)]) + (y + pltpu.roll(y, 1, 1)) + (z + last_z(z))


def sweep(target, v, b, f, w, p, n):
    target[pl.ds(p, n)] = v[pl.ds(p, n)] + w[pl.ds(p, n)] * remainder(b, f, v, p, n)


def body(sizes, src, inx, iny, inz, out_p, out_r, IN, PKs, FYs, FYr, RK, W0, VA, VD, VB, VY, VE, VF, RZ, U0,
         F1, F1S, B1, B1S, W1, X1, Y1, Y1R, Y1S, Z1, U1, F2, F2S, B2, B2S, W2, X2, Y2, Y2R, Y2S, Z2,
         T3s, T3r, G3f, B3s, B3r, G3b, EG, XG, YG, ZG, PD, RR, QQ, XS, send_sem, recv_sem, load_sem, store_sem):
    wide, narrow, ring, group = sizes
    i, j = lax.axis_index("wide"), lax.axis_index("narrow")
    zi, ri = lax.div(i, group), lax.rem(i, group)

    def wide_at(step):
        return lax.rem(i + (step + wide), wide)

    def narrow_at(step):
        return lax.rem(j + (step + narrow), narrow)

    loads = []
    for number, ref in enumerate((inx, iny, inz, src)):
        loads.append(pltpu.make_async_copy(ref, IN.at[number, pl.ds(3, 8), pl.ds(0, 32)], load_sem.at[number]))
        loads[-1].start()

    barrier = pltpu.get_barrier_semaphore()
    partners = [(wide_at(a), narrow_at(b)) for a in (0, 1, -1, 2, -2) for b in (0, 1, -1) if (a, b) != (0, 0)]
    partners += [(i, narrow_at(d)) for d in range(2, narrow - 1)]
    partners += [(lax.rem(zi + d, ring) * group + ri, j) for d in range(1, ring)]
    partners += [(zi * group + lax.rem(ri + d, group), j) for d in range(1, group)]
    for partner in partners:
        pl.semaphore_signal(barrier, inc=1, device_id=partner, device_id_type=MESH)

    sent = []

    def send(source, target, partner):
        number = len(sent)
        copy = pltpu.make_async_remote_copy(
            src_ref=source, dst_ref=target, send_sem=send_sem.at[number], recv_sem=recv_sem.at[number],
            device_id=partner, device_id_type=MESH)
        copy.start()
        sent.append(copy)
        return copy

    def arrive(copies):
        for copy in copies:
            copy.wait_recv()

    def exchange(source, target, stage, own, rows, steps, sides=(0, 1, -1)):
        copies = []
        for a in steps:
            for b in sides:
                if (a, b) == (0, 0):
                    continue
                partner = (wide_at(-a), narrow_at(-b))
                if b == 0:
                    piece = source.at[:, pl.ds(4, own), pl.ds(0, rows)]
                    place = target.at[:, pl.ds(4 + a * own, own), pl.ds(0, rows)]
                else:
                    piece = source.at[:, pl.ds(4, own), pl.ds(rows - 8 if b == -1 else 0, 8)]
                    place = stage.at[0 if b == -1 else 1, :, pl.ds(4 + a * own, own)]
                copies.append(send(piece, place, partner))
        return copies

    near, far = (0, 1, -1), (2, -2)

    tile_row = iota((8, 128), 0)
    row256 = iota((8, 256), 0)

    def merged(stage, field, plane):
        return jnp.where(tile_row < 4, stage[1, field, plane], stage[0, field, plane])

    pl.semaphore_wait(barrier, len(partners))
    first = []
    for number, ref in enumerate((inx, iny, inz, src)):
        more = 3 if number == 0 else 2
        first.append(send(ref.at[pl.ds(8 - more, more)], IN.at[number, pl.ds(3 - more, more), pl.ds(0, 32)], (wide_at(1), j)))
        first.append(send(ref.at[pl.ds(0, 2)], IN.at[number, pl.ds(11, 2), pl.ds(0, 32)], (wide_at(-1), j)))

    for copy in loads:
        copy.wait()

    @pl.loop(0, 4)
    def pack(c):
        for p in (2 * c, 2 * c + 1):
            up = jnp.zeros((8, 256), F32)
            down = jnp.zeros((8, 256), F32)
            for f in range(4):
                mine = (row256 >> 1) == f
                up = jnp.where(mine, pltpu.roll(IN[f, 3 + p, 24:32], (2 * f + 2) % 8, 0), up)
                down = jnp.where(mine, pltpu.roll(IN[f, 3 + p, 0:8], 2 * f, 0), down)
            PKs[0, p] = up
            PKs[1, p] = down

    for p in range(8):
        FYs[p:p + 1] = IN[1, 3 + p, 29:30]

    for side, b in ((0, 1), (1, -1)):
        first.append(send(PKs.at[side], RK.at[side, pl.ds(2, 8)], (i, narrow_at(b))))
    first.append(send(FYs, FYr, (i, narrow_at(1))))
    for side, b in ((0, 1), (1, -1)):
        first.append(send(PKs.at[side, pl.ds(6, 2)], RK.at[side, pl.ds(0, 2)], (wide_at(1), narrow_at(b))))
        first.append(send(PKs.at[side, pl.ds(0, 2)], RK.at[side, pl.ds(10, 2)], (wide_at(-1), narrow_at(b))))

    pairs0 = ones_where((iota((256, 128), 0) >> 1) == iota((256, 128), 1))
    odds0 = ones_where(iota((256, 128), 0) == 2 * iota((256, 128), 1) + 1)
    pairs1 = ones_where((iota((128, 128), 0) >> 1) == iota((128, 128), 1))
    odds1 = ones_where(iota((128, 128), 0) == 2 * iota((128, 128), 1) + 1)
    pairs2 = ones_where((iota((128, 128), 0) >> 1) == (iota((128, 128), 1) & 31))
    odds2 = ones_where(iota((128, 128), 0) == 2 * (iota((128, 128), 1) & 31) + 1)

    def paired(tiles, odd_only=False):
        lanes = tiles[0].shape[1]
        half = tiles[0].shape[0] // 2
        for c, tile in enumerate(tiles):
            for part in range(lanes // 128):
                RZ[part, c, 0:2 * half] = tile[:, 128 * part:128 * (part + 1)]
        below = []
        for c in range(len(tiles)):
            beside = []
            for part in range(lanes // 128):
                odd = RZ[part, c, pl.ds(1, half, stride=2), :]
                beside.append(odd if odd_only else RZ[part, c, pl.ds(0, half, stride=2), :] + odd)
            below.append(jnp.concatenate(beside, axis=1) if len(beside) > 1 else beside[0])
        return jnp.concatenate(below, axis=0)

    def coarse_faces(f, at, target, own, rows, pairs, odds):
        half = rows // 2
        x = [f[0, at + 2 * c + 1, 0:rows] for c in range(own)]
        y = [f[1, at + 2 * c, 0:rows] + f[1, at + 2 * c + 1, 0:rows] for c in range(own)]
        z = [f[2, at + 2 * c, 0:rows] + f[2, at + 2 * c + 1, 0:rows] for c in range(own)]
        for number, (tiles, odd_only, chosen) in enumerate(((x, False, pairs), (y, True, pairs), (z, False, odds))):
            got = picked(paired(tiles, odd_only), chosen)
            for c in range(own):
                target[number, 4 + c, 0:half] = got[c * half:(c + 1) * half]

    coarse_faces(IN, 3, F1, 4, 32, pairs0, odds0)
    faces1 = exchange(F1, F1, F1S, 4, 16, near)
    coarse_faces(F1, 4, F2, 2, 16, pairs1, odds1)

    lane_block = iota((8, 128), 1) >> 5
    both_rows = (tile_row >> 1) == lane_block
    odd_rows = tile_row == 2 * lane_block + 1

    def to_row(tile, chosen, mask):
        got = jnp.where(mask, picked(tile, chosen), 0.0)
        return jnp.broadcast_to(jnp.sum(got, axis=0, keepdims=True), (narrow, 128))

    T3s[0] = to_row(F2[0, 5, 0:8], pairs2, both_rows)
    T3s[1] = to_row(F2[1, 4, 0:8] + F2[1, 5, 0:8], pairs2, odd_rows)
    T3s[2] = to_row(F2[2, 4, 0:8] + F2[2, 5, 0:8], odds2, both_rows)
    gather_f = [send(T3s, T3r.at[j], (i, narrow_at(d))) for d in range(1, narrow)]
    T3r[j] = T3s[...]

    arrive(first)
    has_low, has_high = j > 0, j < narrow - 1

    @pl.loop(0, 12)
    def unpack(q):
        low, high = RK[0, q], RK[1, q]
        for f in range(4):
            from_high = pltpu.roll(high, (8 - 2 * f) % 8, 0)
            from_low = pltpu.roll(low, (14 - 2 * f) % 8, 0)
            if f == 1:
                from_low = jnp.where(has_low, from_low, 0.0)
            IN[f, q + 1, 32:40] = jnp.where(row256 < 2, from_high, jnp.where(row256 >= 6, from_low, 0.0))

    IN[0, 0, 32:40] = jnp.zeros((8, 256), F32)
    for p in range(8):
        IN[1, 3 + p, 37:38] = jnp.where(has_low, FYr[p:p + 1], 0.0)

    @pl.when(i == 0)
    def _():
        IN[0, 2] = jnp.zeros((40, 256), F32)

    def inside(rows, lanes, own_rows, reach):
        row = iota((rows, lanes), 0)
        mask = (row < own_rows) | ((row < own_rows + reach) & has_high) | ((row >= rows - reach) & has_low)
        return mask

    def plane_in(p, own):
        return (i * own + p >= 0) & (i * own + p < own * wide)

    rows_in0 = inside(40, 256, 32, 2)
    weight_in = jnp.where(rows_in0, relax, 0.0)

    @pl.loop(-1, 5)
    def start0(c):
        p = 2 * c
        w = jnp.where(plane_in(p, 8), weight_in, 0.0)[None] / diagonal(IN, p + 3, 2)
        W0[pl.ds(p + 3, 2)] = w
        VA[pl.ds(p + 3, 2)] = w * IN[3, pl.ds(p + 3, 2)]

    @pl.loop(0, 5)
    def down0(c):
        sweep(VD, VA, IN.at[3], IN, W0, 2 * c + 2, 2)

    @pl.loop(0, 4)
    def restrict0(c):
        both = remainder(IN.at[3], IN, VD, 2 * c + 3, 2)
        VE[c, 0:32] = both[0, :32] + both[1, :32]

    got = paired([VE[c, 0:32] for c in range(4)])
    got = picked(got, pairs0)
    for c in range(4):
        B1[0, 4 + c, 0:16] = got[16 * c:16 * (c + 1)]
    rhs1 = exchange(B1, B1, B1S, 4, 16, near)
    faces2 = exchange(F2, F2, F2S, 2, 8, near + far)

    arrive(gather_f)
    sub = iota((narrow, 128), 0)

    def assembled(parts):
        tile = parts[0]
        for n in range(1, narrow):
            tile = jnp.where(sub == n, parts[n], tile)
        return tile

    for f in range(3):
        G3f[f, zi, ri] = assembled([T3r[n, f] for n in range(narrow)])
    gather_f = [send(G3f.at[:, zi, ri], G3f.at[:, zi, ri], (lax.rem(zi + d, ring) * group + ri, j)) for d in range(1, ring)]

    def finish_faces(f, stage, planes, rows):
        for field in range(3):
            tile = jnp.where(tile_row[None] < 4, stage[1, field], stage[0, field])
            if field == 1:
                tile = jnp.where(((tile_row < 4) | has_low)[None], tile, 0.0)
            f[field, :, rows:rows + 8] = tile

        @pl.when(i == 0)
        def _():
            f[0, 3] = jnp.zeros(f.shape[2:], F32)

        if planes == 10:
            @pl.when(i == 1)
            def _():
                f[0, 1] = jnp.zeros(f.shape[2:], F32)

    arrive(faces1)
    finish_faces(F1, F1S, 12, 16)
    rows_in1 = inside(24, 128, 16, 4)
    weight_in1 = jnp.where(rows_in1, relax, 0.0)

    for p, n in ((-3, 3), (0, 4), (4, 4)):
        W1[p + 4:p + 4 + n] = jnp.where(plane_in(p, 4), weight_in1, 0.0)[None] / diagonal(F1, p + 4, n)

    arrive(rhs1)
    B1[0, :, 16:24] = jnp.where(tile_row[None] < 4, B1S[1, 0], B1S[0, 0])
    X1[2:10] = W1[2:10] * B1[0, 2:10]
    for p in (-1, 2):
        sweep(Y1.at[0], X1, B1.at[0], F1, W1, p + 4, 3)

    rest = remainder(B1.at[0], F1, Y1.at[0], 4, 4)
    got = paired([rest[2 * c, :16] + rest[2 * c + 1, :16] for c in range(2)])
    got = picked(got, pairs1)
    for c in range(2):
        B2[0, 4 + c, 0:8] = got[8 * c:8 * (c + 1)]
    rhs2 = exchange(B2, B2, B2S, 2, 8, near)

    arrive(gather_f)
    gather_f = [send(G3f.at[:, :, ri], G3f.at[:, :, ri], (zi * group + lax.rem(ri + d, group), j)) for d in range(2, group, 2)]

    arrive(faces2)
    finish_faces(F2, F2S, 10, 8)
    rows_in2 = inside(16, 128, 8, 4) & (iota((16, 128), 1) < 64)

    weights = relax / diagonal(F2, 1, 9)
    for p in range(-3, 6):
        W2[p + 4] = jnp.where(rows_in2 & plane_in(p, 2), weights[p + 3], 0.0)

    arrive(rhs2)
    B2[0, 2:8, 8:16] = jnp.where(tile_row[None] < 4, B2S[1, 0, 2:8], B2S[0, 0, 2:8])
    X2[2:8] = W2[2:8] * B2[0, 2:8]
    sweep(Y2.at[0], X2, B2.at[0], F2, W2, 3, 4)
    rest = remainder(B2.at[0], F2, Y2.at[0], 4, 2)
    B3s[...] = to_row(rest[0, :8] + rest[1, :8], pairs2, both_rows)
    gather_b = [send(B3s, B3r.at[j], (i, narrow_at(d))) for d in range(1, narrow)]
    B3r[j] = B3s[...]

    back2 = exchange(Y2, Y2R, Y2S, 2, 8, near + far, (0,)) + exchange(B2, B2, B2S, 2, 8, far, (0,))
    back1 = exchange(Y1, Y1R, Y1S, 4, 16, near, (0,))
    background = [
        send(VD.at[pl.ds(8, 3), pl.ds(0, 32)], VB.at[pl.ds(0, 3)], (wide_at(1), j)),
        send(VD.at[pl.ds(3, 3), pl.ds(0, 32)], VB.at[pl.ds(3, 3)], (wide_at(-1), j))]
    arrive(gather_b)
    G3b[zi, ri] = assembled([B3r[n] for n in range(narrow)])
    gather_b = [send(G3b.at[zi, ri], G3b.at[zi, ri], (lax.rem(zi + d, ring) * group + ri, j)) for d in range(1, ring)]

    back2 += exchange(Y2, Y2R, Y2S, 2, 8, near + far, (1, -1)) + exchange(B2, B2, B2S, 2, 8, far, (1, -1))
    back1 += exchange(Y1, Y1R, Y1S, 4, 16, near, (1, -1))
    for side, b, row in ((0, 1, 24), (1, -1, 0)):
        background.append(send(VD.at[pl.ds(3, 8), pl.ds(row, 8)], VY.at[side, pl.ds(3, 8)], (i, narrow_at(b))))
        background.append(send(VD.at[pl.ds(8, 3), pl.ds(row, 8)], VY.at[side, pl.ds(0, 3)], (wide_at(1), narrow_at(b))))
        background.append(send(VD.at[pl.ds(3, 3), pl.ds(row, 8)], VY.at[side, pl.ds(11, 3)], (wide_at(-1), narrow_at(b))))

    arrive(gather_f)
    core = lax.rem(i, 2)
    sibling = (i + 1 - 2 * core, j)
    gather_f = [send(G3f.at[:, :, 2 * c + core], G3f.at[:, :, 2 * c + core], sibling) for c in range(group // 2)]
    arrive(gather_f)
    block3 = iota((narrow, 128), 1) >> 5
    lane3 = iota((narrow, 128), 1) & 31
    last_y = (sub == narrow - 1) & (block3 == 3)
    last_lane = lane3 == 31

    XG[0] = jnp.zeros((narrow, 128), F32)

    @pl.loop(0, ring)
    def masks3(a):
        y, z = G3f[1, a], G3f[2, a]
        planes = pl.ds(a * group, group)
        XG[pl.ds(a * group + 1, group)] = G3f[0, a]
        EG[planes] = jnp.where(last_y[None], y, 0.0) + jnp.where(last_lane[None], z, 0.0)
        YG[planes] = jnp.where(last_y[None], 0.0, y)
        ZG[planes] = jnp.where(last_lane[None], 0.0, z)

    arrive(gather_b)
    gather_b = [send(G3b.at[:, ri], G3b.at[:, ri], (zi * group + lax.rem(ri + d, group), j)) for d in range(1, group)]

    for p in (0, 1, wide + 2, wide + 3):
        PD[p] = jnp.zeros((narrow, 128), F32)
    for p in range(5):
        XS[p] = jnp.zeros((narrow, 128), F32)
    arrive(gather_b)

    def next_y3(cells):
        moved = pltpu.roll(cells, 96, 2)
        return jnp.where(block3[None] == 3, pltpu.roll(moved, narrow - 1, 1), moved)

    def last_y3(cells):
        moved = pltpu.roll(cells, 32, 2)
        return jnp.where(block3[None] == 0, pltpu.roll(moved, 1, 1), moved)

    def summed(total):
        return jnp.sum(jnp.sum(total, axis=0, keepdims=True), axis=1, keepdims=True)

    zero3 = jnp.zeros((narrow, 128), F32)
    total = zero3
    for a in range(ring):
        r = G3b[a]
        PD[2 + a * group:2 + (a + 1) * group] = r
        RR[a * group:(a + 1) * group] = r
        total = total + jnp.sum(r * r, axis=0)
    norm_first = summed(total)

    def curvature(keep):
        total = zero3
        for a in range(ring):
            p = a * group
            here = PD[p + 2:p + 2 + group]
            high = XG[p + 1:p + 1 + group] * (here - PD[p + 3:p + 3 + group])
            low = XG[p:p + group] * (PD[p + 1:p + 1 + group] - here)
            along_y = YG[p:p + group] * (here - next_y3(here))
            along_z = ZG[p:p + group] * (here - pltpu.roll(here, 127, 2))
            q = (EG[p:p + group] * here + (high - low)) + (
                (along_y - last_y3(along_y)) + (along_z - pltpu.roll(along_z, 1, 2)))
            if keep:
                QQ[p:p + group] = q
            total = total + jnp.sum(here * q, axis=0)
        return summed(total)

    def iteration(counter, norm_now):
        alpha = norm_now / curvature(True)
        for p in range(5):
            XS[p] = XS[p] + alpha * PD[i + p]
        total = zero3
        for a in range(ring):
            planes = slice(a * group, (a + 1) * group)
            r = RR[planes] - alpha * QQ[planes]
            RR[planes] = r
            total = total + jnp.sum(r * r, axis=0)
        norm_next = summed(total)
        beta = norm_next / norm_now
        for a in range(ring):
            p = a * group
            PD[p + 2:p + 2 + group] = RR[p:p + group] + beta * PD[p + 2:p + 2 + group]
        return norm_next

    norm_now = lax.fori_loop(0, CGI - 1, iteration, norm_first)
    alpha = norm_now / curvature(False)
    for p in range(5):
        XS[p] = XS[p] + alpha * PD[i + p]

    row16 = iota((16, 128), 0)
    wanted = ((row16 & 7) >> 1) == (iota((16, 128), 1) >> 5)
    spread2 = ones_where(((iota((128, 128), 1) >> 1) == (iota((128, 128), 0) & 31)) & (iota((128, 128), 1) < 64))
    high_j, low_j = jnp.minimum(j + 1, narrow - 1), jnp.maximum(j - 1, 0)
    spread = []
    for p in range(5):
        middle = jnp.broadcast_to(XS[p, pl.ds(j, 1), :], (16, 128))
        above = jnp.broadcast_to(XS[p, pl.ds(high_j, 1), :], (16, 128))
        below = jnp.broadcast_to(XS[p, pl.ds(low_j, 1), :], (16, 128))
        x = jnp.where(row16 < 8, middle, jnp.where(row16 < 12, above, below))
        spread.append(jnp.where(wanted, x, 0.0))
    spread = picked(jnp.concatenate(spread, axis=0), spread2)
    arrive(back2)
    reach2 = inside(16, 128, 8, 4)
    for p in (0, 1, 8, 9):
        B2[0, p, 8:16] = merged(B2S, 0, p)
    for p in range(-4, 6):
        own = Y2[0, p + 4, 0:8] if 0 <= p < 2 else Y2R[0, p + 4, 0:8]
        x = jnp.concatenate([own, merged(Y2S, 0, p + 4)], axis=0)
        c = (p + 4) // 2
        x = x + spread[16 * c:16 * (c + 1)]
        X2[p + 4] = jnp.where(reach2 & plane_in(p, 2), x, 0.0)
    sweep(Z2, X2, B2.at[0], F2, W2, 1, 8)
    sweep(X2, Z2, B2.at[0], F2, W2, 2, 6)

    spread1 = ones_where((iota((128, 128), 1) >> 1) == iota((128, 128), 0))
    spread = picked(jnp.concatenate([X2[p + 4] for p in range(-2, 4)], axis=0), spread1)
    for c in range(6):
        U1[c, pl.ds(0, 16, stride=2), :] = spread[16 * c:16 * (c + 1)]
        U1[c, pl.ds(1, 16, stride=2), :] = spread[16 * c:16 * (c + 1)]
    arrive(back1)
    reach1 = inside(24, 128, 16, 4)
    for p in range(-4, 8):
        c = (p + 4) // 2
        own = Y1[0, p + 4, 0:16] if 0 <= p < 4 else Y1R[0, p + 4, 0:16]
        edge = merged(Y1S, 0, p + 4) + jnp.where(tile_row < 4, U1[c, 16:24], U1[c, 24:32])
        x = jnp.concatenate([own + U1[c, 0:16], edge], axis=0)
        X1[p + 4] = jnp.where(reach1 & plane_in(p, 4), x, 0.0)

    for p in (-3, 2):
        sweep(Z1, X1, B1.at[0], F1, W1, p + 4, 5)
    for p in (-2, 2):
        sweep(X1, Z1, B1.at[0], F1, W1, p + 4, 4)

    spread0 = ones_where((iota((128, 256), 1) >> 1) == iota((128, 256), 0))
    spread = picked(jnp.concatenate([X1[p + 4] for p in range(-2, 6)], axis=0), spread0)
    for c in range(8):
        for half in (0, 128):
            part = spread[24 * c:24 * (c + 1), half:half + 128]
            U0[half // 128, c, pl.ds(0, 24, stride=2), :] = part
            U0[half // 128, c, pl.ds(1, 24, stride=2), :] = part
    arrive(background)
    reach0 = inside(40, 256, 32, 4)

    def corrected(p, own):
        c = lax.div(p + 4, 2)
        u = jnp.concatenate([U0[0, c], U0[1, c]], axis=1)
        edge = jnp.where(row256 < 4, VY[1, p + 3] + u[32:40], VY[0, p + 3] + u[40:48])
        x = jnp.concatenate([own + u[0:32], edge], axis=0)
        return jnp.where(reach0 & plane_in(p, 8), x, 0.0)

    @pl.loop(0, 8)
    def correct0(p):
        VE[p + 3] = corrected(p, VD[p + 3, 0:32])

    @pl.loop(0, 3)
    def correct0_ends(p):
        VE[p] = corrected(p - 3, VB[p])
        VE[p + 11] = corrected(p + 8, VB[p + 3])

    @pl.loop(0, 6)
    def up0(c):
        sweep(VA, VE, IN.at[3], IN, W0, 2 * c + 1, 2)

    @pl.loop(0, 5)
    def up0_again(c):
        sweep(VF, VA, IN.at[3], IN, W0, 2 * c + 2, 2)

    store = pltpu.make_async_copy(VF.at[pl.ds(3, 8), pl.ds(0, 32)], out_p, store_sem.at[0])
    store.start()

    @pl.loop(0, 4)
    def rest0(c):
        VE[pl.ds(2 * c, 2)] = remainder(IN.at[3], IN, VF, 2 * c + 3, 2)

    store_r = pltpu.make_async_copy(VE.at[pl.ds(0, 8), pl.ds(0, 32)], out_r, store_sem.at[1])
    store_r.start()
    for copy in sent:
        copy.wait_send()
    store.wait()
    store_r.wait()


def shards(sizes, source, face_x, face_y, face_z):
    wide, narrow, ring, group = sizes
    shape = jax.ShapeDtypeStruct((8, 32, 256), F32)

    def V(*size):
        return pltpu.VMEM(size, F32)

    scratch = [
        V(4, 13, 40, 256), V(2, 8, 8, 256), V(8, 256), V(8, 256), V(2, 12, 8, 256),
        V(14, 40, 256), V(14, 40, 256), V(14, 40, 256), V(6, 32, 256), V(2, 14, 8, 256), V(14, 40, 256), V(14, 40, 256),
        V(2, 4, 32, 128), V(2, 8, 48, 128),
        V(3, 12, 24, 128), V(2, 3, 12, 8, 128), V(1, 12, 24, 128), V(2, 1, 12, 8, 128), V(12, 24, 128), V(12, 24, 128),
        V(1, 12, 24, 128), V(1, 12, 24, 128), V(2, 1, 12, 8, 128), V(12, 24, 128), V(6, 32, 128),
        V(3, 10, 16, 128), V(2, 3, 10, 8, 128), V(1, 10, 16, 128), V(2, 1, 10, 8, 128), V(10, 16, 128), V(10, 16, 128),
        V(1, 10, 16, 128), V(1, 10, 16, 128), V(2, 1, 10, 8, 128), V(10, 16, 128),
        V(3, narrow, 128), V(narrow, 3, narrow, 128), V(3, ring, group, narrow, 128),
        V(narrow, 128), V(narrow, narrow, 128), V(ring, group, narrow, 128), V(wide, narrow, 128),
        V(wide + 1, narrow, 128), V(wide, narrow, 128), V(wide, narrow, 128),
        V(wide + 4, narrow, 128), V(wide, narrow, 128), V(wide, narrow, 128), V(5, narrow, 128),
        pltpu.SemaphoreType.DMA((144,)), pltpu.SemaphoreType.DMA((144,)), pltpu.SemaphoreType.DMA((4,)),
        pltpu.SemaphoreType.DMA((2,)),
    ]
    anywhere = pl.BlockSpec(memory_space=pl.ANY)
    return pl.pallas_call(
        functools.partial(body, sizes),
        out_shape=(shape, shape),
        in_specs=[anywhere] * 4,
        out_specs=(anywhere, anywhere),
        scratch_shapes=scratch,
        compiler_params=pltpu.CompilerParams(collective_id=0, has_side_effects=True, vmem_limit_bytes=60 * 1024 * 1024),
    )(source, face_x, face_y, face_z)


def solution(mesh):
    wide, narrow = mesh.shape["wide"], mesh.shape["narrow"]
    group = 8 if wide == 64 else wide // 2
    spec = P("wide", "narrow", None)
    return jax.shard_map(
        functools.partial(shards, (wide, narrow, wide // group, group)),
        mesh=mesh,
        in_specs=(spec,) * 4,
        out_specs=(spec, spec),
        check_vma=False,
    )
```

```python
import functools

import jax
import jax.numpy as jnp
from jax import lax
from jax.experimental import pallas as pl
from jax.experimental.pallas import tpu as pltpu
from jax.sharding import PartitionSpec as P

CGI = 6
relax = 0.8
MESH = pl.DeviceIdType.MESH
F32 = jnp.float32
BF16 = jnp.bfloat16


def iota(shape, dim):
    return lax.broadcasted_iota(jnp.int32, shape, dim)


def picked(values, chosen):
    high = values.astype(BF16)
    rest = values - high.astype(F32)
    middle = rest.astype(BF16)
    low = (rest - middle.astype(F32)).astype(BF16)
    product = functools.partial(jnp.dot, preferred_element_type=F32)
    return product(high, chosen) + product(middle, chosen) + product(low, chosen)


def ones_where(condition):
    return jnp.where(condition, 1.0, 0.0).astype(BF16)


def next_z(cells):
    lanes = cells.shape[-1]
    lane = iota(cells.shape[:-1] + (128,), len(cells.shape) - 1)
    axis = len(cells.shape) - 1
    if lanes == 128:
        return jnp.where(lane == 127, 0.0, pltpu.roll(cells, 127, axis))
    first = pltpu.roll(cells[..., :128], 127, axis)
    second = pltpu.roll(cells[..., 128:], 127, axis)
    return jnp.concatenate([jnp.where(lane == 127, second, first), jnp.where(lane == 127, 0.0, second)], axis=axis)


def last_z(cells):
    lanes = cells.shape[-1]
    lane = iota(cells.shape[:-1] + (128,), len(cells.shape) - 1)
    axis = len(cells.shape) - 1
    if lanes == 128:
        return jnp.where(lane == 0, 0.0, pltpu.roll(cells, 1, axis))
    first = pltpu.roll(cells[..., :128], 1, axis)
    second = pltpu.roll(cells[..., 128:], 1, axis)
    return jnp.concatenate([jnp.where(lane == 0, 0.0, first), jnp.where(lane == 0, first, second)], axis=axis)


def remainder(b, f, v, p, n=1):
    here = v[pl.ds(p, n)]
    rows = here.shape[1]
    flow = f[0, pl.ds(p, n)] * (v[pl.ds(p + 1, n)] - here) - f[0, pl.ds(p - 1, n)] * (here - v[pl.ds(p - 1, n)])
    along = f[1, pl.ds(p, n)] * (pltpu.roll(here, rows - 1, 1) - here)
    flow = flow + (along - pltpu.roll(along, 1, 1))
    along = f[2, pl.ds(p, n)] * (next_z(here) - here)
    flow = flow + (along - last_z(along))
    return b[pl.ds(p, n)] + flow


def diagonal(f, p, n=1):
    x, y, z = f[0, pl.ds(p, n)], f[1, pl.ds(p, n)], f[2, pl.ds(p, n)]
    return (x + f[0, pl.ds(p - 1, n)]) + (y + pltpu.roll(y, 1, 1)) + (z + last_z(z))


def sweep(target, v, b, f, w, p, n):
    target[pl.ds(p, n)] = v[pl.ds(p, n)] + w[pl.ds(p, n)] * remainder(b, f, v, p, n)


def body(sizes, src, inx, iny, inz, out_p, out_r, IN, PKs, FYs, FYr, RK, W0, VA, VD, VB, VY, VE, VF, RZ, U0,
         F1, F1S, B1, B1S, W1, X1, Y1, Y1R, Y1S, Z1, U1, F2, F2S, B2, B2S, W2, X2, Y2, Y2R, Y2S, Z2,
         T3s, T3r, G3f, B3s, B3r, G3b, EG, XG, YG, ZG, PD, RR, QQ, XS, send_sem, recv_sem, load_sem, store_sem):
    wide, narrow, ring, group = sizes
    i, j = lax.axis_index("wide"), lax.axis_index("narrow")
    zi, ri = lax.div(i, group), lax.rem(i, group)

    def wide_at(step):
        return lax.rem(i + (step + wide), wide)

    def narrow_at(step):
        return lax.rem(j + (step + narrow), narrow)

    loads = []
    for number, ref in enumerate((inx, iny, inz, src)):
        loads.append(pltpu.make_async_copy(ref, IN.at[number, pl.ds(3, 8), pl.ds(0, 32)], load_sem.at[number]))
        loads[-1].start()

    barrier = pltpu.get_barrier_semaphore()
    partners = [(wide_at(a), narrow_at(b)) for a in (0, 1, -1, 2, -2) for b in (0, 1, -1) if (a, b) != (0, 0)]
    partners += [(i, narrow_at(d)) for d in range(2, narrow - 1)]
    partners += [(lax.rem(zi + d, ring) * group + ri, j) for d in range(1, ring)]
    partners += [(zi * group + lax.rem(ri + d, group), j) for d in range(1, group)]
    for partner in partners:
        pl.semaphore_signal(barrier, inc=1, device_id=partner, device_id_type=MESH)

    sent = []

    def send(source, target, partner):
        number = len(sent)
        copy = pltpu.make_async_remote_copy(
            src_ref=source, dst_ref=target, send_sem=send_sem.at[number], recv_sem=recv_sem.at[number],
            device_id=partner, device_id_type=MESH)
        copy.start()
        sent.append(copy)
        return copy

    def arrive(copies):
        for copy in copies:
            copy.wait_recv()

    def exchange(source, target, stage, own, rows, steps, sides=(0, 1, -1)):
        copies = []
        for a in steps:
            for b in sides:
                if (a, b) == (0, 0):
                    continue
                partner = (wide_at(-a), narrow_at(-b))
                if b == 0:
                    piece = source.at[:, pl.ds(4, own), pl.ds(0, rows)]
                    place = target.at[:, pl.ds(4 + a * own, own), pl.ds(0, rows)]
                else:
                    piece = source.at[:, pl.ds(4, own), pl.ds(rows - 8 if b == -1 else 0, 8)]
                    place = stage.at[0 if b == -1 else 1, :, pl.ds(4 + a * own, own)]
                copies.append(send(piece, place, partner))
        return copies

    near, far = (0, 1, -1), (2, -2)

    tile_row = iota((8, 128), 0)
    row256 = iota((8, 256), 0)

    def merged(stage, field, plane):
        return jnp.where(tile_row < 4, stage[1, field, plane], stage[0, field, plane])

    pl.semaphore_wait(barrier, len(partners))
    first = []
    for number, ref in enumerate((inx, iny, inz, src)):
        more = 3 if number == 0 else 2
        first.append(send(ref.at[pl.ds(8 - more, more)], IN.at[number, pl.ds(3 - more, more), pl.ds(0, 32)], (wide_at(1), j)))
        first.append(send(ref.at[pl.ds(0, 2)], IN.at[number, pl.ds(11, 2), pl.ds(0, 32)], (wide_at(-1), j)))

    for copy in loads:
        copy.wait()

    @pl.loop(0, 4)
    def pack(c):
        for p in (2 * c, 2 * c + 1):
            up = jnp.zeros((8, 256), F32)
            down = jnp.zeros((8, 256), F32)
            for f in range(4):
                mine = (row256 >> 1) == f
                up = jnp.where(mine, pltpu.roll(IN[f, 3 + p, 24:32], (2 * f + 2) % 8, 0), up)
                down = jnp.where(mine, pltpu.roll(IN[f, 3 + p, 0:8], 2 * f, 0), down)
            PKs[0, p] = up
            PKs[1, p] = down

    for p in range(8):
        FYs[p:p + 1] = IN[1, 3 + p, 29:30]

    for side, b in ((0, 1), (1, -1)):
        first.append(send(PKs.at[side], RK.at[side, pl.ds(2, 8)], (i, narrow_at(b))))
    first.append(send(FYs, FYr, (i, narrow_at(1))))
    for side, b in ((0, 1), (1, -1)):
        first.append(send(PKs.at[side, pl.ds(6, 2)], RK.at[side, pl.ds(0, 2)], (wide_at(1), narrow_at(b))))
        first.append(send(PKs.at[side, pl.ds(0, 2)], RK.at[side, pl.ds(10, 2)], (wide_at(-1), narrow_at(b))))

    pairs0 = ones_where((iota((256, 128), 0) >> 1) == iota((256, 128), 1))
    odds0 = ones_where(iota((256, 128), 0) == 2 * iota((256, 128), 1) + 1)
    pairs1 = ones_where((iota((128, 128), 0) >> 1) == iota((128, 128), 1))
    odds1 = ones_where(iota((128, 128), 0) == 2 * iota((128, 128), 1) + 1)
    pairs2 = ones_where((iota((128, 128), 0) >> 1) == (iota((128, 128), 1) & 31))
    odds2 = ones_where(iota((128, 128), 0) == 2 * (iota((128, 128), 1) & 31) + 1)

    def paired(tiles, odd_only=False):
        lanes = tiles[0].shape[1]
        half = tiles[0].shape[0] // 2
        for c, tile in enumerate(tiles):
            for part in range(lanes // 128):
                RZ[part, c, 0:2 * half] = tile[:, 128 * part:128 * (part + 1)]
        below = []
        for c in range(len(tiles)):
            beside = []
            for part in range(lanes // 128):
                odd = RZ[part, c, pl.ds(1, half, stride=2), :]
                beside.append(odd if odd_only else RZ[part, c, pl.ds(0, half, stride=2), :] + odd)
            below.append(jnp.concatenate(beside, axis=1) if len(beside) > 1 else beside[0])
        return jnp.concatenate(below, axis=0)

    def coarse_faces(f, at, target, own, rows, pairs, odds):
        half = rows // 2
        x = [f[0, at + 2 * c + 1, 0:rows] for c in range(own)]
        y = [f[1, at + 2 * c, 0:rows] + f[1, at + 2 * c + 1, 0:rows] for c in range(own)]
        z = [f[2, at + 2 * c, 0:rows] + f[2, at + 2 * c + 1, 0:rows] for c in range(own)]
        for number, (tiles, odd_only, chosen) in enumerate(((x, False, pairs), (y, True, pairs), (z, False, odds))):
            got = picked(paired(tiles, odd_only), chosen)
            for c in range(own):
                target[number, 4 + c, 0:half] = got[c * half:(c + 1) * half]

    coarse_faces(IN, 3, F1, 4, 32, pairs0, odds0)
    faces1 = exchange(F1, F1, F1S, 4, 16, near)
    coarse_faces(F1, 4, F2, 2, 16, pairs1, odds1)

    lane_block = iota((8, 128), 1) >> 5
    both_rows = (tile_row >> 1) == lane_block
    odd_rows = tile_row == 2 * lane_block + 1

    def to_row(tile, chosen, mask):
        got = jnp.where(mask, picked(tile, chosen), 0.0)
        return jnp.broadcast_to(jnp.sum(got, axis=0, keepdims=True), (narrow, 128))

    T3s[0] = to_row(F2[0, 5, 0:8], pairs2, both_rows)
    T3s[1] = to_row(F2[1, 4, 0:8] + F2[1, 5, 0:8], pairs2, odd_rows)
    T3s[2] = to_row(F2[2, 4, 0:8] + F2[2, 5, 0:8], odds2, both_rows)
    gather_f = [send(T3s, T3r.at[j], (i, narrow_at(d))) for d in range(1, narrow)]
    T3r[j] = T3s[...]

    arrive(first)
    has_low, has_high = j > 0, j < narrow - 1

    @pl.loop(0, 12)
    def unpack(q):
        low, high = RK[0, q], RK[1, q]
        for f in range(4):
            from_high = pltpu.roll(high, (8 - 2 * f) % 8, 0)
            from_low = pltpu.roll(low, (14 - 2 * f) % 8, 0)
            if f == 1:
                from_low = jnp.where(has_low, from_low, 0.0)
            IN[f, q + 1, 32:40] = jnp.where(row256 < 2, from_high, jnp.where(row256 >= 6, from_low, 0.0))

    IN[0, 0, 32:40] = jnp.zeros((8, 256), F32)
    for p in range(8):
        IN[1, 3 + p, 37:38] = jnp.where(has_low, FYr[p:p + 1], 0.0)

    @pl.when(i == 0)
    def _():
        IN[0, 2] = jnp.zeros((40, 256), F32)

    def inside(rows, lanes, own_rows, reach):
        row = iota((rows, lanes), 0)
        mask = (row < own_rows) | ((row < own_rows + reach) & has_high) | ((row >= rows - reach) & has_low)
        return mask

    def plane_in(p, own):
        return (i * own + p >= 0) & (i * own + p < own * wide)

    rows_in0 = inside(40, 256, 32, 2)
    weight_in = jnp.where(rows_in0, relax, 0.0)

    @pl.loop(-1, 5)
    def start0(c):
        p = 2 * c
        w = jnp.where(plane_in(p, 8), weight_in, 0.0)[None] / diagonal(IN, p + 3, 2)
        W0[pl.ds(p + 3, 2)] = w
        VA[pl.ds(p + 3, 2)] = w * IN[3, pl.ds(p + 3, 2)]

    for c in range(5):
        sweep(VD, VA, IN.at[3], IN, W0, 2 * c + 2, 2)

    @pl.loop(0, 4)
    def restrict0(c):
        both = remainder(IN.at[3], IN, VD, 2 * c + 3, 2)
        VE[c, 0:32] = both[0, :32] + both[1, :32]

    got = paired([VE[c, 0:32] for c in range(4)])
    got = picked(got, pairs0)
    for c in range(4):
        B1[0, 4 + c, 0:16] = got[16 * c:16 * (c + 1)]
    rhs1 = exchange(B1, B1, B1S, 4, 16, near)
    faces2 = exchange(F2, F2, F2S, 2, 8, near + far)

    arrive(gather_f)
    sub = iota((narrow, 128), 0)

    def assembled(parts):
        tile = parts[0]
        for n in range(1, narrow):
            tile = jnp.where(sub == n, parts[n], tile)
        return tile

    for f in range(3):
        G3f[f, zi, ri] = assembled([T3r[n, f] for n in range(narrow)])
    gather_f = [send(G3f.at[:, zi, ri], G3f.at[:, zi, ri], (lax.rem(zi + d, ring) * group + ri, j)) for d in range(1, ring)]

    def finish_faces(f, stage, planes, rows):
        for field in range(3):
            tile = jnp.where(tile_row[None] < 4, stage[1, field], stage[0, field])
            if field == 1:
                tile = jnp.where(((tile_row < 4) | has_low)[None], tile, 0.0)
            f[field, :, rows:rows + 8] = tile

        @pl.when(i == 0)
        def _():
            f[0, 3] = jnp.zeros(f.shape[2:], F32)

        if planes == 10:
            @pl.when(i == 1)
            def _():
                f[0, 1] = jnp.zeros(f.shape[2:], F32)

    arrive(faces1)
    finish_faces(F1, F1S, 12, 16)
    rows_in1 = inside(24, 128, 16, 4)
    weight_in1 = jnp.where(rows_in1, relax, 0.0)

    for p, n in ((-3, 3), (0, 4), (4, 4)):
        W1[p + 4:p + 4 + n] = jnp.where(plane_in(p, 4), weight_in1, 0.0)[None] / diagonal(F1, p + 4, n)

    arrive(rhs1)
    B1[0, :, 16:24] = jnp.where(tile_row[None] < 4, B1S[1, 0], B1S[0, 0])
    X1[2:10] = W1[2:10] * B1[0, 2:10]
    for p in (-1, 2):
        sweep(Y1.at[0], X1, B1.at[0], F1, W1, p + 4, 3)

    rest = remainder(B1.at[0], F1, Y1.at[0], 4, 4)
    got = paired([rest[2 * c, :16] + rest[2 * c + 1, :16] for c in range(2)])
    got = picked(got, pairs1)
    for c in range(2):
        B2[0, 4 + c, 0:8] = got[8 * c:8 * (c + 1)]
    rhs2 = exchange(B2, B2, B2S, 2, 8, near)
    early = len(sent)

    arrive(gather_f)
    gather_f = [send(G3f.at[:, :, ri], G3f.at[:, :, ri], (zi * group + lax.rem(ri + d, group), j)) for d in range(2, group, 2)]

    arrive(faces2)
    finish_faces(F2, F2S, 10, 8)
    rows_in2 = inside(16, 128, 8, 4) & (iota((16, 128), 1) < 64)

    weights = relax / diagonal(F2, 1, 9)
    for p in range(-3, 6):
        W2[p + 4] = jnp.where(rows_in2 & plane_in(p, 2), weights[p + 3], 0.0)

    arrive(rhs2)
    B2[0, 2:8, 8:16] = jnp.where(tile_row[None] < 4, B2S[1, 0, 2:8], B2S[0, 0, 2:8])
    X2[2:8] = W2[2:8] * B2[0, 2:8]
    sweep(Y2.at[0], X2, B2.at[0], F2, W2, 3, 4)
    rest = remainder(B2.at[0], F2, Y2.at[0], 4, 2)
    B3s[...] = to_row(rest[0, :8] + rest[1, :8], pairs2, both_rows)
    gather_b = [send(B3s, B3r.at[j], (i, narrow_at(d))) for d in range(1, narrow)]
    B3r[j] = B3s[...]

    back2 = exchange(Y2, Y2R, Y2S, 2, 8, near + far, (0,)) + exchange(B2, B2, B2S, 2, 8, far, (0,))
    back1 = exchange(Y1, Y1R, Y1S, 4, 16, near, (0,))
    background = [
        send(VD.at[pl.ds(8, 3), pl.ds(0, 32)], VB.at[pl.ds(0, 3)], (wide_at(1), j)),
        send(VD.at[pl.ds(3, 3), pl.ds(0, 32)], VB.at[pl.ds(3, 3)], (wide_at(-1), j))]
    arrive(gather_b)
    G3b[zi, ri] = assembled([B3r[n] for n in range(narrow)])
    gather_b = [send(G3b.at[zi, ri], G3b.at[zi, ri], (lax.rem(zi + d, ring) * group + ri, j)) for d in range(1, ring)]

    back2 += exchange(Y2, Y2R, Y2S, 2, 8, near + far, (1, -1)) + exchange(B2, B2, B2S, 2, 8, far, (1, -1))
    back1 += exchange(Y1, Y1R, Y1S, 4, 16, near, (1, -1))
    for side, b, row in ((0, 1, 24), (1, -1, 0)):
        background.append(send(VD.at[pl.ds(3, 8), pl.ds(row, 8)], VY.at[side, pl.ds(3, 8)], (i, narrow_at(b))))
        background.append(send(VD.at[pl.ds(8, 3), pl.ds(row, 8)], VY.at[side, pl.ds(0, 3)], (wide_at(1), narrow_at(b))))
        background.append(send(VD.at[pl.ds(3, 3), pl.ds(row, 8)], VY.at[side, pl.ds(11, 3)], (wide_at(-1), narrow_at(b))))

    arrive(gather_f)
    core = lax.rem(i, 2)
    sibling = (i + 1 - 2 * core, j)
    gather_f = [send(G3f.at[:, :, 2 * c + core], G3f.at[:, :, 2 * c + core], sibling) for c in range(group // 2)]
    arrive(gather_f)
    block3 = iota((narrow, 128), 1) >> 5
    lane3 = iota((narrow, 128), 1) & 31
    last_y = (sub == narrow - 1) & (block3 == 3)
    last_lane = lane3 == 31

    XG[0] = jnp.zeros((narrow, 128), F32)

    @pl.loop(0, ring)
    def masks3(a):
        y, z = G3f[1, a], G3f[2, a]
        planes = pl.ds(a * group, group)
        XG[pl.ds(a * group + 1, group)] = G3f[0, a]
        EG[planes] = jnp.where(last_y[None], y, 0.0) + jnp.where(last_lane[None], z, 0.0)
        YG[planes] = jnp.where(last_y[None], 0.0, y)
        ZG[planes] = jnp.where(last_lane[None], 0.0, z)

    arrive(gather_b)
    gather_b = [send(G3b.at[:, ri], G3b.at[:, ri], (zi * group + lax.rem(ri + d, group), j)) for d in range(1, group)]

    for p in (0, 1, wide + 2, wide + 3):
        PD[p] = jnp.zeros((narrow, 128), F32)
    for p in range(5):
        XS[p] = jnp.zeros((narrow, 128), F32)
    for copy in sent[:early]:
        copy.wait_send()
    arrive(gather_b)

    def next_y3(cells):
        moved = pltpu.roll(cells, 96, 2)
        return jnp.where(block3[None] == 3, pltpu.roll(moved, narrow - 1, 1), moved)

    def last_y3(cells):
        moved = pltpu.roll(cells, 32, 2)
        return jnp.where(block3[None] == 0, pltpu.roll(moved, 1, 1), moved)

    def summed(total):
        return jnp.sum(jnp.sum(total, axis=0, keepdims=True), axis=1, keepdims=True)

    zero3 = jnp.zeros((narrow, 128), F32)
    total = zero3
    for a in range(ring):
        r = G3b[a]
        PD[2 + a * group:2 + (a + 1) * group] = r
        RR[a * group:(a + 1) * group] = r
        total = total + jnp.sum(r * r, axis=0)
    norm_first = summed(total)

    def curvature(beta):
        def turn(a):
            p = a * group
            PD[p + 2:p + 2 + group] = RR[p:p + group] + beta * PD[p + 2:p + 2 + group]

        if beta is not None:
            turn(0)
        total = zero3
        for a in range(ring):
            if beta is not None and a < ring - 1:
                turn(a + 1)
            p = a * group
            here = PD[p + 2:p + 2 + group]
            high = XG[p + 1:p + 1 + group] * (here - PD[p + 3:p + 3 + group])
            low = XG[p:p + group] * (PD[p + 1:p + 1 + group] - here)
            along_y = YG[p:p + group] * (here - next_y3(here))
            along_z = ZG[p:p + group] * (here - pltpu.roll(here, 127, 2))
            q = (EG[p:p + group] * here + (high - low)) + (
                (along_y - last_y3(along_y)) + (along_z - pltpu.roll(along_z, 1, 2)))
            QQ[p:p + group] = q
            total = total + jnp.sum(here * q, axis=0)
        return summed(total)

    def iteration(counter, carry):
        norm_now, curved = carry
        alpha = norm_now / curved
        for p in range(5):
            XS[p] = XS[p] + alpha * PD[i + p]
        total = zero3
        for a in range(ring):
            planes = slice(a * group, (a + 1) * group)
            r = RR[planes] - alpha * QQ[planes]
            RR[planes] = r
            total = total + jnp.sum(r * r, axis=0)
        norm_next = summed(total)
        return norm_next, curvature(norm_next / norm_now)

    norm_now, curved = lax.fori_loop(0, CGI - 1, iteration, (norm_first, curvature(None)))
    alpha = norm_now / curved
    for p in range(5):
        XS[p] = XS[p] + alpha * PD[i + p]

    row16 = iota((16, 128), 0)
    wanted = ((row16 & 7) >> 1) == (iota((16, 128), 1) >> 5)
    spread2 = ones_where(((iota((128, 128), 1) >> 1) == (iota((128, 128), 0) & 31)) & (iota((128, 128), 1) < 64))
    high_j, low_j = jnp.minimum(j + 1, narrow - 1), jnp.maximum(j - 1, 0)
    spread = []
    for p in range(5):
        middle = jnp.broadcast_to(XS[p, pl.ds(j, 1), :], (16, 128))
        above = jnp.broadcast_to(XS[p, pl.ds(high_j, 1), :], (16, 128))
        below = jnp.broadcast_to(XS[p, pl.ds(low_j, 1), :], (16, 128))
        x = jnp.where(row16 < 8, middle, jnp.where(row16 < 12, above, below))
        spread.append(jnp.where(wanted, x, 0.0))
    spread = picked(jnp.concatenate(spread, axis=0), spread2)
    arrive(back2)
    reach2 = inside(16, 128, 8, 4)
    for p in (0, 1, 8, 9):
        B2[0, p, 8:16] = merged(B2S, 0, p)
    for p in range(-4, 6):
        own = Y2[0, p + 4, 0:8] if 0 <= p < 2 else Y2R[0, p + 4, 0:8]
        x = jnp.concatenate([own, merged(Y2S, 0, p + 4)], axis=0)
        c = (p + 4) // 2
        x = x + spread[16 * c:16 * (c + 1)]
        X2[p + 4] = jnp.where(reach2 & plane_in(p, 2), x, 0.0)
    sweep(Z2, X2, B2.at[0], F2, W2, 1, 8)
    sweep(X2, Z2, B2.at[0], F2, W2, 2, 6)

    spread1 = ones_where((iota((128, 128), 1) >> 1) == iota((128, 128), 0))
    spread = picked(jnp.concatenate([X2[p + 4] for p in range(-2, 4)], axis=0), spread1)
    for c in range(6):
        U1[c, pl.ds(0, 16, stride=2), :] = spread[16 * c:16 * (c + 1)]
        U1[c, pl.ds(1, 16, stride=2), :] = spread[16 * c:16 * (c + 1)]
    arrive(back1)
    reach1 = inside(24, 128, 16, 4)
    for p in range(-4, 8):
        c = (p + 4) // 2
        own = Y1[0, p + 4, 0:16] if 0 <= p < 4 else Y1R[0, p + 4, 0:16]
        edge = merged(Y1S, 0, p + 4) + jnp.where(tile_row < 4, U1[c, 16:24], U1[c, 24:32])
        x = jnp.concatenate([own + U1[c, 0:16], edge], axis=0)
        X1[p + 4] = jnp.where(reach1 & plane_in(p, 4), x, 0.0)

    for p in (-3, 2):
        sweep(Z1, X1, B1.at[0], F1, W1, p + 4, 5)
    for p in (-2, 2):
        sweep(X1, Z1, B1.at[0], F1, W1, p + 4, 4)

    spread0 = ones_where((iota((128, 256), 1) >> 1) == iota((128, 256), 0))
    spread = picked(jnp.concatenate([X1[p + 4] for p in range(-2, 6)], axis=0), spread0)
    for c in range(8):
        for half in (0, 128):
            part = spread[24 * c:24 * (c + 1), half:half + 128]
            U0[half // 128, c, pl.ds(0, 24, stride=2), :] = part
            U0[half // 128, c, pl.ds(1, 24, stride=2), :] = part
    arrive(background)
    reach0 = inside(40, 256, 32, 4)

    def corrected(p, own):
        c = lax.div(p + 4, 2)
        u = jnp.concatenate([U0[0, c], U0[1, c]], axis=1)
        edge = jnp.where(row256 < 4, VY[1, p + 3] + u[32:40], VY[0, p + 3] + u[40:48])
        x = jnp.concatenate([own + u[0:32], edge], axis=0)
        return jnp.where(reach0 & plane_in(p, 8), x, 0.0)

    @pl.loop(0, 8)
    def correct0(p):
        VE[p + 3] = corrected(p, VD[p + 3, 0:32])

    @pl.loop(0, 3)
    def correct0_ends(p):
        VE[p] = corrected(p - 3, VB[p])
        VE[p + 11] = corrected(p + 8, VB[p + 3])

    for c in range(6):
        sweep(VA, VE, IN.at[3], IN, W0, 2 * c + 1, 2)

    for c in range(5):
        sweep(VF, VA, IN.at[3], IN, W0, 2 * c + 2, 2)

    store = pltpu.make_async_copy(VF.at[pl.ds(3, 8), pl.ds(0, 32)], out_p, store_sem.at[0])
    store.start()

    for c in range(4):
        VE[pl.ds(2 * c, 2)] = remainder(IN.at[3], IN, VF, 2 * c + 3, 2)

    store_r = pltpu.make_async_copy(VE.at[pl.ds(0, 8), pl.ds(0, 32)], out_r, store_sem.at[1])
    store_r.start()
    for copy in sent[early:]:
        copy.wait_send()
    store.wait()
    store_r.wait()


def shards(sizes, source, face_x, face_y, face_z):
    wide, narrow, ring, group = sizes
    shape = jax.ShapeDtypeStruct((8, 32, 256), F32)

    def V(*size):
        return pltpu.VMEM(size, F32)

    scratch = [
        V(4, 13, 40, 256), V(2, 8, 8, 256), V(8, 256), V(8, 256), V(2, 12, 8, 256),
        V(14, 40, 256), V(14, 40, 256), V(14, 40, 256), V(6, 32, 256), V(2, 14, 8, 256), V(14, 40, 256), V(14, 40, 256),
        V(2, 4, 32, 128), V(2, 8, 48, 128),
        V(3, 12, 24, 128), V(2, 3, 12, 8, 128), V(1, 12, 24, 128), V(2, 1, 12, 8, 128), V(12, 24, 128), V(12, 24, 128),
        V(1, 12, 24, 128), V(1, 12, 24, 128), V(2, 1, 12, 8, 128), V(12, 24, 128), V(6, 32, 128),
        V(3, 10, 16, 128), V(2, 3, 10, 8, 128), V(1, 10, 16, 128), V(2, 1, 10, 8, 128), V(10, 16, 128), V(10, 16, 128),
        V(1, 10, 16, 128), V(1, 10, 16, 128), V(2, 1, 10, 8, 128), V(10, 16, 128),
        V(3, narrow, 128), V(narrow, 3, narrow, 128), V(3, ring, group, narrow, 128),
        V(narrow, 128), V(narrow, narrow, 128), V(ring, group, narrow, 128), V(wide, narrow, 128),
        V(wide + 1, narrow, 128), V(wide, narrow, 128), V(wide, narrow, 128),
        V(wide + 4, narrow, 128), V(wide, narrow, 128), V(wide, narrow, 128), V(5, narrow, 128),
        pltpu.SemaphoreType.DMA((144,)), pltpu.SemaphoreType.DMA((144,)), pltpu.SemaphoreType.DMA((4,)),
        pltpu.SemaphoreType.DMA((2,)),
    ]
    anywhere = pl.BlockSpec(memory_space=pl.ANY)
    return pl.pallas_call(
        functools.partial(body, sizes),
        out_shape=(shape, shape),
        in_specs=[anywhere] * 4,
        out_specs=(anywhere, anywhere),
        scratch_shapes=scratch,
        compiler_params=pltpu.CompilerParams(collective_id=0, has_side_effects=True, vmem_limit_bytes=60 * 1024 * 1024),
    )(source, face_x, face_y, face_z)


def solution(mesh):
    wide, narrow = mesh.shape["wide"], mesh.shape["narrow"]
    group = 8 if wide == 64 else wide // 2
    spec = P("wide", "narrow", None)
    return jax.shard_map(
        functools.partial(shards, (wide, narrow, wide // group, group)),
        mesh=mesh,
        in_specs=(spec,) * 4,
        out_specs=(spec, spec),
        check_vma=False,
    )
```
